256 devices in a mesh: tm: 64 (over x_hi, y, z), height: 4 (over x_lo, core).
Axes of the slice: x: 4 (x_hi: 2, x_lo: 2; x = x_hi * 2 + x_lo), y: 4, z: 8, core: 2. Of those that a mesh axis runs over, the one named last changes fastest.
Arguments:
- query_states: bfloat16 [128, 64, 16, 1536], P('tm', 'height'), may hold values from -9 to 9
- key_states: bfloat16 [128, 64, 16, 1536], P('tm', 'height'), may hold values from -9 to 9
- value_states: bfloat16 [128, 64, 16, 1536], P('tm', 'height'), may hold values from -6 to 6
- shifts: int32 [2], replicated, may hold values from 1 to 7
- conv_kernel: float32 [27, 1536], replicated, may hold values from -0.5 to 0.5
- out_weight: bfloat16 [1536, 3072], replicated, may hold values from -0.15625 to 0.15625
Outputs:
- block_out: bfloat16 [128, 64, 16, 3072], P('tm', 'height')
The draws below stay inside these ranges and needn't reach their ends.
All inputs are finite; a program needn't handle non-finite values.
Results may differ from the reference program's by a relative error of at most 0.0059.
Values may be sent and summed in bfloat16 or wider, within the bound.
A program may use at most 192 MiB of HBM per device.

```python
import math
import jax
import jax.numpy as jnp
from jax import lax

HEADS = 12
HEAD_DIM = 128
D = 3072
WL = 16
NF = 128
NH = 64


def draw_query_states(key, part):
    key = jax.random.fold_in(key, 3)
    noise_part = jnp.clip(jax.random.normal(key, (NF, NH, WL, HEADS * HEAD_DIM), jnp.float32), -4.0, 4.0)
    values = noise_part
    return values.astype(jnp.bfloat16)


def draw_key_states(key, part):
    key = jax.random.fold_in(key, 4)
    noise_part = jnp.clip(jax.random.normal(key, (NF, NH, WL, HEADS * HEAD_DIM), jnp.float32), -4.0, 4.0)
    values = noise_part
    return values.astype(jnp.bfloat16)


def level_of(rng, dims, cuts, low, high):
    def one(dim, blocks):
        draws = jax.random.uniform(jax.random.fold_in(jax.random.fold_in(rng, 6), dim), (blocks,), jnp.float32, low / len(cuts), high / len(cuts))
        return jnp.repeat(jnp.exp(draws), dims[dim] // blocks).reshape((-1,) + (1,) * (len(dims) - dim - 1))

    factor_of = one(*cuts[0])
    for cut in cuts[1:]:
        factor_of = factor_of * one(*cut)
    return factor_of


def bell_draw(rng, shape, width, bound, cuts=(), kind=jnp.bfloat16):
    loudness = level_of(rng, shape, cuts, -0.22, 0.18) if cuts else 1.0
    values = jax.random.normal(rng, shape, jnp.float32) * width * loudness
    return jnp.minimum(jnp.maximum(values, -bound), bound).astype(kind)


def setup_inputs(seed: int = 0) -> dict:
    arg_keys = jax.random.split(jax.random.key(seed), 7)
    return {
        "query_states": draw_query_states(jax.random.fold_in(arg_keys[6], 71), 0),
        "key_states": draw_key_states(jax.random.fold_in(arg_keys[6], 71), 0),
        "value_states": bell_draw(arg_keys[2], (NF, NH, WL, HEADS * HEAD_DIM), 1.0, 6.0, ((0, 64), (1, 4))),
        "shifts": jax.random.randint(arg_keys[3], (2,), 1, 8).astype(jnp.int32),
        "conv_kernel": bell_draw(arg_keys[4], (27, HEADS * HEAD_DIM), 0.08, 0.5, (), jnp.float32),
        "out_weight": bell_draw(arg_keys[5], (HEADS * HEAD_DIM, D), (HEADS * HEAD_DIM) ** -0.5, 0.15625),
    }


def soft_weights(scores):
    row_max = lax.optimization_barrier(jnp.max(scores, axis=-1, keepdims=True))
    spread = jnp.exp(scores - row_max)
    return (spread / lax.optimization_barrier(jnp.sum(spread, axis=-1, keepdims=True))).astype(jnp.bfloat16)

def conv_positions(value_states, conv_kernel):
    frame_count, row_count, col_count = (value_states.shape[0], value_states.shape[1], value_states.shape[2])
    padded = jnp.pad(value_states.astype(jnp.float32), ((1, 1), (1, 1), (1, 1), (0, 0)))
    summed = jnp.zeros(value_states.shape, jnp.float32)
    for offset in range(27):
        delta_t, delta_r, delta_c = (offset // 9, offset // 3 % 3, offset % 3)
        summed = summed + conv_kernel[offset] * padded[delta_t:delta_t + frame_count, delta_r:delta_r + row_count, delta_c:delta_c + col_count]
    return summed

def attend_block(query_block, key_block, value_block):
    row_count, col_count = (query_block.shape[1], query_block.shape[2])

    def window_tokens(values):
        values = values.astype(jnp.float32).reshape(2, row_count // 8, 8, col_count // 8, 8, HEADS, HEAD_DIM)
        return values.transpose(1, 3, 5, 0, 2, 4, 6).reshape(row_count // 8, col_count // 8, HEADS, 128, HEAD_DIM)
    scores = jnp.einsum('awhqd,awhkd->awhqk', window_tokens(query_block), window_tokens(key_block)) * (1.0 / math.sqrt(HEAD_DIM))
    weights = soft_weights(scores)
    result = jnp.einsum('awhqk,awhkd->awhqd', weights.astype(jnp.float32), window_tokens(value_block)).astype(jnp.bfloat16)
    result = result.reshape(row_count // 8, col_count // 8, HEADS, 2, 8, 8, HEAD_DIM)
    return result.transpose(3, 0, 4, 1, 5, 2, 6).reshape(2, row_count, col_count, HEADS * HEAD_DIM)

def roll_axes(values, frame_by, row_by, col_by):
    values = jnp.roll(values, frame_by, axis=0)
    values = jnp.roll(values, row_by, axis=1)
    return jnp.roll(values, col_by, axis=2)

def reference(query_states, key_states, value_states, shifts, conv_kernel, out_weight):
    shift_rows, shift_cols = (shifts[0], shifts[1])
    rolled_query = roll_axes(query_states, -1, -shift_rows, -shift_cols)
    rolled_key = roll_axes(key_states, -1, -shift_rows, -shift_cols)
    rolled_value = roll_axes(value_states, -1, -shift_rows, -shift_cols)

    def window_group(group_idx):
        first_frame = group_idx * 2
        pieces = [lax.dynamic_slice_in_dim(source, first_frame, 2, 0) for source in (rolled_query, rolled_key, rolled_value)]
        return attend_block(pieces[0], pieces[1], pieces[2])
    attended = lax.map(window_group, jnp.arange(NF // 2, dtype=jnp.int32))
    attended = attended.reshape(NF, NH, WL, HEADS * HEAD_DIM)
    attended = roll_axes(attended, 1, shift_rows, shift_cols)
    position_term = conv_positions(value_states, conv_kernel)
    mixed_in = (attended.astype(jnp.float32) + position_term).astype(jnp.bfloat16)
    block_out = jnp.dot(mixed_in.reshape(NF * NH * WL, HEADS * HEAD_DIM), out_weight, preferred_element_type=jnp.float32)
    return block_out.astype(jnp.bfloat16).reshape(NF, NH, WL, D)
```

```python
import functools
import math

import jax
import jax.numpy as jnp
from jax import lax
from jax.experimental import pallas as pl
from jax.experimental.pallas import tpu as pltpu
from jax.sharding import PartitionSpec as P

HEAD_DIM = 128
MESH = pl.DeviceIdType.MESH
NEG = -1e30
SCALE = math.log2(math.e) / math.sqrt(HEAD_DIM)


def kernel(
    nt, heads_per, chunks, tile,
    shifts, q_hbm, k_hbm, v_hbm, cw, w_hbm, out_hbm,
    q, kv, hb, asm, mo, w, acc, mixed, ostage, ob, vext, colbias, same,
    lsem, zs, zr, asend, arecv, ms, mr, fs, fr, hs, hr, osem,
):
    lanes_per = heads_per * HEAD_DIM
    t = lax.axis_index("tm")
    h = lax.axis_index("height")
    core = lax.rem(h, 2)
    nxt = (lax.rem(t + 1, nt), h)
    prv = (lax.rem(t + nt - 1, nt), h)
    buddy = (t, h + 1 - 2 * core)
    across = (t, lax.rem(h + 2, 4))
    m_rows = pl.ds(8 * core, 8)
    h_rows = pl.ds(8 - 8 * core, 8)
    s_row = shifts[0]
    s_col = shifts[1]

    def lanes_of(g):
        return pl.ds(pl.multiple_of(g * lanes_per, 128), lanes_per)

    def remote(src, dst, ssem, rsem, dev):
        return pltpu.make_async_remote_copy(
            src_ref=src, dst_ref=dst, send_sem=ssem, recv_sem=rsem, device_id=dev, device_id_type=MESH
        )

    loads = [
        pltpu.make_async_copy(k_hbm, kv.at[0, 1:3], lsem.at[0]),
        pltpu.make_async_copy(v_hbm, kv.at[1, 1:3], lsem.at[1]),
        pltpu.make_async_copy(q_hbm, q, lsem.at[2]),
        pltpu.make_async_copy(w_hbm, w, lsem.at[3]),
    ]
    for load in loads:
        load.start()

    bar = pltpu.get_barrier_semaphore()
    for dev in (nxt, prv, buddy, across):
        pl.semaphore_signal(bar, inc=1, device_id=dev, device_id_type=MESH)
    pl.semaphore_wait(bar, 4)

    part_frames = (pl.ds(1, 2), pl.ds(0, 1), pl.ds(3, 1))

    def z_copy(phase, way, tensor, g):
        rows = (m_rows, h_rows)[phase]
        src = (k_hbm, v_hbm)[tensor].at[1 - way, rows, :, lanes_of(g)]
        dst = kv.at[tensor, 3 * way, rows, :, lanes_of(g)]
        return remote(src, dst, zs.at[phase, way, tensor, g], zr.at[phase, way, tensor, g], (nxt, prv)[way])

    def asm_copy(part, g):
        fr_ = part_frames[part]
        return remote(
            kv.at[1 - core, fr_, m_rows, :, lanes_of(g)], asm.at[fr_, :, :, lanes_of(g)],
            asend.at[part, g], arecv.at[part, g], buddy,
        )

    def x_copy(part, g):
        fr_ = part_frames[part]
        return remote(
            mo.at[fr_, :, :, lanes_of(g)], hb.at[core, fr_, 0:8, :, lanes_of(g)],
            ms.at[part, g], mr.at[part, g], across,
        )

    def fwd_copy(part, g):
        fr_ = part_frames[part]
        return remote(
            hb.at[core, fr_, 0:8, :, lanes_of(g)], hb.at[core, fr_, 0:8, :, lanes_of(g)],
            fs.at[part, g], fr.at[part, g], buddy,
        )

    def halo_copy(part, g):
        fr_ = part_frames[part]
        return remote(
            kv.at[:, fr_, h_rows, :, lanes_of(g)], hb.at[:, fr_, 8:16, :, lanes_of(g)],
            hs.at[part, g], hr.at[part, g], buddy,
        )

    def assemble(part, g):
        for frame in ((1, 2), (0,), (3,))[part]:
            for j in range(8):
                ours = (s_row <= j).astype(jnp.int32) == core
                mine = kv[core, frame, 8 * core + j, :, lanes_of(g)]
                mo[frame, j, :, lanes_of(g)] = jnp.where(ours, mine, asm[frame, j, :, lanes_of(g)])

    loads[0].wait()
    loads[1].wait()

    @pl.loop(0, chunks)
    def _(g):
        asm_copy(0, g).start()

    for phase in range(2):
        @pl.loop(0, chunks)
        def _(g):
            for way in range(2):
                for tensor in range(2):
                    z_copy(phase, way, tensor, g).start()

    @pl.loop(0, chunks)
    def _(g):
        halo_copy(0, g).start()

    qi = lax.broadcasted_iota(jnp.int32, (128, 256), 0)
    ki = lax.broadcasted_iota(jnp.int32, (128, 256), 1)
    q_win = ((qi % 16 - s_col + 16) % 16) // 8
    k_win = ((ki % 16 - s_col + 16) % 16) // 8
    colbias[...] = jnp.where(q_win == k_win, 0.0, NEG)
    q_low = (qi // 16 >= s_row).astype(jnp.int32)
    k_low = (ki % 128 // 16 >= s_row).astype(jnp.int32)
    same[...] = (q_low == k_low).astype(jnp.float32)

    @pl.loop(0, chunks)
    def _(g):
        asm_copy(0, g).wait_recv()
        assemble(0, g)
        x_copy(0, g).start()

    def corner_send(g):
        for part in (1, 2):
            asm_copy(part, g).wait_recv()
            assemble(part, g)
            x_copy(part, g).start()

    @pl.loop(0, chunks + 1)
    def _(g):
        @pl.when(g < chunks)
        def _():
            for way in range(2):
                for tensor in range(2):
                    z_copy(0, way, tensor, g).wait_recv()
            for part in (1, 2):
                asm_copy(part, g).start()
            x_copy(0, g).wait_recv()
            fwd_copy(0, g).start()

        @pl.when(g > 0)
        def _():
            corner_send(g - 1)

    loads[2].wait()
    loads[3].wait()

    low = [s_row <= j for j in range(8)]

    def slots(ref, lead, picks, lanes):
        return [
            jnp.where(pick, ref[(*lead, j, slice(None), lanes)], ref[(*lead, 8 + j, slice(None), lanes)])
            for j, pick in enumerate(picks)
        ]

    r_one = low
    r_two = [s_row > j for j in range(8)]
    r_halo = [(s_row <= j).astype(jnp.int32) != core for j in range(8)]

    def weights_of(scores):
        z = scores * SCALE + colbias[...]
        e = jnp.exp2(z - jnp.max(z, axis=1, keepdims=True))
        return e, 1.0 / jnp.sum(e, axis=1, keepdims=True)

    def dot_t(a, b):
        return lax.dot_general(a, b, (((1,), (1,)), ((), ())), preferred_element_type=jnp.float32)

    def dot(a, b):
        return jnp.dot(a, b, preferred_element_type=jnp.float32)

    def attend(frame, lanes):
        frames = (0, 1) if frame == 0 else (2, 3)

        def keys(ref, tensor, rows):
            return jnp.concatenate([x for f in frames for x in slots(ref, (tensor, f), rows, lanes)], axis=0)

        q_one = jnp.concatenate(slots(q, (frame,), r_one, lanes), axis=0)
        e, inv = weights_of(dot_t(q_one, keys(kv, 0, r_one)))
        one = (dot(e.astype(jnp.bfloat16), keys(kv, 1, r_one)) * inv).astype(jnp.bfloat16)

        q_two = jnp.concatenate(slots(q, (frame,), r_two, lanes), axis=0)
        pick = same[...] > 0.5
        e, inv = weights_of(
            jnp.where(pick, dot_t(q_two, keys(kv, 0, r_two)), dot_t(q_two, keys(hb, 0, r_halo)))
        )
        near = jnp.where(pick, e, 0.0).astype(jnp.bfloat16)
        far = jnp.where(pick, 0.0, e).astype(jnp.bfloat16)
        two = ((dot(near, keys(kv, 1, r_two)) + dot(far, keys(hb, 1, r_halo))) * inv).astype(jnp.bfloat16)
        for j in range(8):
            a = one[16 * j : 16 * j + 16]
            b = two[16 * j : 16 * j + 16]
            ob[frame, j] = jnp.where(low[j], a, b)
            ob[frame, 8 + j] = jnp.where(low[j], b, a)

    def convolve(lanes, mixed_lanes):
        keep_frame = (t > 0, None, None, t < nt - 1)
        for f in range(4):
            top = hb[1, f, 7 + 8 * core, :, lanes].astype(jnp.float32)
            bottom = hb[1, f, 8 - 8 * core, :, lanes].astype(jnp.float32)
            body = kv[1, f, :, :, lanes].astype(jnp.float32)
            top = jnp.where(h > 0, top, 0.0)
            bottom = jnp.where(h < 3, bottom, 0.0)
            if keep_frame[f] is not None:
                top = jnp.where(keep_frame[f], top, 0.0)
                bottom = jnp.where(keep_frame[f], bottom, 0.0)
                body = jnp.where(keep_frame[f], body, 0.0)
            vext[f, 0] = top
            vext[f, 17] = bottom
            vext[f, 1:17] = body
        col = lax.broadcasted_iota(jnp.int32, (4, 16, 128), 1)
        for f in range(2):
            @pl.loop(0, 4)
            def _(rb):
                sums = [jnp.zeros((4, 16, 128), jnp.float32) for _ in range(3)]
                for dt in range(3):
                    for dr in range(3):
                        slab = vext[f + dt, pl.ds(4 * rb + dr, 4)]
                        for dc in range(3):
                            tap = 9 * dt + 3 * dr + dc
                            sums[dc] = sums[dc] + cw[tap : tap + 1, lanes][None] * slab
                left = jnp.where(col > 0, pltpu.roll(sums[0], 1, 1), 0.0)
                right = jnp.where(col < 15, pltpu.roll(sums[2], 15, 1), 0.0)
                term = sums[1] + left + right
                win = ob[f, pl.ds(4 * rb, 4)].astype(jnp.float32)
                mixed[f, pl.ds(4 * rb, 4), :, mixed_lanes] = (win + term).astype(jnp.bfloat16)

    def out_copy(i):
        cols = pl.ds(pl.multiple_of(i * tile, tile), tile)
        return pltpu.make_async_copy(ostage.at[:, cols], out_hbm.at[:, cols], osem.at[i])

    tiles = acc.shape[1] // tile

    def project(g):
        left = mixed[...].reshape(512, lanes_per)

        @pl.loop(0, tiles)
        def _(i):
            cols = pl.ds(pl.multiple_of(i * tile, tile), tile)
            part = dot(left, w[pl.ds(pl.multiple_of(g * lanes_per, 128), lanes_per), cols])

            @pl.when(g == 0)
            def _():
                acc[:, cols] = part

            @pl.when((g > 0) & (g < chunks - 1))
            def _():
                acc[:, cols] = acc[:, cols] + part

            @pl.when(g == chunks - 1)
            def _():
                ostage[:, cols] = (acc[:, cols] + part).astype(jnp.bfloat16)
                out_copy(i).start()

    def compute(g):
        halo_copy(0, g).wait_recv()
        fwd_copy(0, g).wait_recv()
        for part in (1, 2):
            halo_copy(part, g).wait_recv()
            fwd_copy(part, g).wait_recv()

        @pl.loop(0, heads_per)
        def _(i):
            lanes = pl.ds(pl.multiple_of(g * lanes_per + i * 128, 128), 128)
            for frame in range(2):
                attend(frame, lanes)
            convolve(lanes, pl.ds(pl.multiple_of(i * 128, 128), 128))

        project(g)

    @pl.loop(0, chunks + 1)
    def _(g):
        @pl.when(g < chunks)
        def _():
            for way in range(2):
                for tensor in range(2):
                    z_copy(1, way, tensor, g).wait_recv()
            for part in (1, 2):
                halo_copy(part, g).start()
            for part in (1, 2):
                x_copy(part, g).wait_recv()
                fwd_copy(part, g).start()

        @pl.when(g > 0)
        def _():
            compute(g - 1)

    @pl.loop(0, chunks)
    def _(g):
        for phase in range(2):
            for way in range(2):
                for tensor in range(2):
                    z_copy(phase, way, tensor, g).wait_send()
        for part in range(3):
            asm_copy(part, g).wait_send()
            x_copy(part, g).wait_send()
            fwd_copy(part, g).wait_send()
            halo_copy(part, g).wait_send()

    @pl.loop(0, tiles)
    def _(i):
        out_copy(i).wait()


def body(nt, query_states, key_states, value_states, shifts, conv_kernel, out_weight):
    frames, rows, cols, channels = query_states.shape
    width = out_weight.shape[1]
    heads = channels // HEAD_DIM
    heads_per = 2 if heads % 2 == 0 and heads > 2 else 1
    chunks = heads // heads_per
    tile = 256
    any_spec = pl.BlockSpec(memory_space=pl.ANY)
    dma = pltpu.SemaphoreType.DMA
    bf16 = jnp.bfloat16
    out = pl.pallas_call(
        functools.partial(kernel, nt, heads_per, chunks, tile),
        out_shape=jax.ShapeDtypeStruct((frames * rows * cols, width), bf16),
        in_specs=[
            pl.BlockSpec(memory_space=pltpu.SMEM),
            any_spec, any_spec, any_spec,
            pl.BlockSpec(memory_space=pltpu.VMEM),
            any_spec,
        ],
        out_specs=any_spec,
        scratch_shapes=[
            pltpu.VMEM((2, 16, 16, channels), bf16),
            pltpu.VMEM((2, 4, 16, 16, channels), bf16),
            pltpu.VMEM((2, 4, 16, 16, channels), bf16),
            pltpu.VMEM((4, 8, 16, channels), bf16),
            pltpu.VMEM((4, 8, 16, channels), bf16),
            pltpu.VMEM((channels, width), bf16),
            pltpu.VMEM((512, width), jnp.float32),
            pltpu.VMEM((2, 16, 16, heads_per * HEAD_DIM), bf16),
            pltpu.VMEM((512, width), bf16),
            pltpu.VMEM((2, 16, 16, HEAD_DIM), bf16),
            pltpu.VMEM((4, 18, 16, HEAD_DIM), jnp.float32),
            pltpu.VMEM((128, 256), jnp.float32),
            pltpu.VMEM((128, 256), jnp.float32),
            dma((4,)),
            dma((2, 2, 2, chunks)), dma((2, 2, 2, chunks)),
            dma((3, chunks)), dma((3, chunks)),
            dma((3, chunks)), dma((3, chunks)),
            dma((3, chunks)), dma((3, chunks)),
            dma((3, chunks)), dma((3, chunks)),
            dma((width // tile,)),
        ],
        compiler_params=pltpu.CompilerParams(
            collective_id=0, has_side_effects=True, vmem_limit_bytes=60 * 2**20
        ),
        name="window_block",
    )(shifts, query_states, key_states, value_states, conv_kernel, out_weight)
    return out.reshape(frames, rows, cols, width)


def solution(mesh):
    in_specs = (
        P("tm", "height", None, None),
        P("tm", "height", None, None),
        P("tm", "height", None, None),
        P(),
        P(),
        P(),
    )
    out_specs = P("tm", "height", None, None)
    return jax.shard_map(
        functools.partial(body, mesh.shape["tm"]), mesh=mesh, in_specs=in_specs, out_specs=out_specs, check_vma=False
    )
```

```python
import functools
import math

import jax
import jax.numpy as jnp
from jax import lax
from jax.experimental import pallas as pl
from jax.experimental.pallas import tpu as pltpu
from jax.sharding import PartitionSpec as P

HEAD_DIM = 128
MESH = pl.DeviceIdType.MESH
NEG = -1e30
SCALE = math.log2(math.e) / math.sqrt(HEAD_DIM)


def kernel(
    nt, chunks, lag, lead, early, relayed,
    shifts, q_hbm, k_hbm, v_hbm, cw, out_hbm,
    q, kv, hb, asm, mo, mixed, ob, vext, colbias, same, rb,
    lsem, zs, zr, asend, arecv, ms, mr, fs, fr, hs, hr, rs, rr, osem,
):
    t = lax.axis_index("tm")
    h = lax.axis_index("height")
    core = lax.rem(h, 2)
    nxt = (lax.rem(t + 1, nt), h)
    prv = (lax.rem(t + nt - 1, nt), h)
    buddy = (t, h + 1 - 2 * core)
    across = (t, lax.rem(h + 2, 4))
    m_rows = pl.ds(8 * core, 8)
    h_rows = pl.ds(8 - 8 * core, 8)
    s_row = shifts[0]
    s_col = shifts[1]

    def lanes_of(g):
        return pl.ds(pl.multiple_of(g * HEAD_DIM, HEAD_DIM), HEAD_DIM)

    def remote(src, dst, ssem, rsem, dev):
        return pltpu.make_async_remote_copy(
            src_ref=src, dst_ref=dst, send_sem=ssem, recv_sem=rsem, device_id=dev, device_id_type=MESH
        )

    loads = [
        pltpu.make_async_copy(k_hbm, kv.at[0, 1:3], lsem.at[0]),
        pltpu.make_async_copy(v_hbm, kv.at[1, 1:3], lsem.at[1]),
        pltpu.make_async_copy(q_hbm, q, lsem.at[2]),
    ]
    for load in loads:
        load.start()

    greet = [(None, dev) for dev in (nxt, prv, buddy, across)]
    if relayed:
        half, nz = nt // 2, nt // 8
        base = t // half * half
        other = half - base
        y = t % half // nz
        first, last = t % half == 0, t % half == half - 1
        middle = (y == 1) | (y == 2)
        relay_up = (t % nz == 0) & middle
        relay_down = (t % nz == nz - 1) & middle
        relay = relay_up | relay_down
        slot_way = jnp.where(relay_up, 0, 1)
        target = jnp.where(relay_up, other, other + half - 1)
        for p in (1, 2):
            greet.append((last, (base + nz * p, h)))
            greet.append((first, (other + nz * p, h)))
            greet.append((first, (base + nz * p + nz - 1, h)))
            greet.append((last, (other + nz * p + nz - 1, h)))
        greet.append((relay_up, (base + half - 1, h)))
        greet.append((relay_up, (other, h)))
        greet.append((relay_down, (base, h)))
        greet.append((relay_down, (other + half - 1, h)))

    bar = pltpu.get_barrier_semaphore()
    met = 0
    for cond, dev in greet:
        if cond is None:
            pl.semaphore_signal(bar, inc=1, device_id=dev, device_id_type=MESH)
            met = met + 1
        else:
            @pl.when(cond)
            def _():
                pl.semaphore_signal(bar, inc=1, device_id=dev, device_id_type=MESH)
            met = met + jnp.where(cond, 1, 0)
    pl.semaphore_wait(bar, met)

    part_frames = (pl.ds(1, 2), pl.ds(0, 1), pl.ds(3, 1))

    def z_copy(phase, way, tensor, g):
        rows = (m_rows, h_rows)[phase]
        src = (k_hbm, v_hbm)[tensor].at[1 - way, rows, :, lanes_of(g)]
        dst = kv.at[tensor, 3 * way, rows, :, lanes_of(g)]
        return remote(src, dst, zs.at[phase, way, tensor, g], zr.at[phase, way, tensor, g], (nxt, prv)[way])

    def z_start(phase, way, tensor, g):
        if not relayed:
            z_copy(phase, way, tensor, g).start()
            return
        p = g % 3
        detour = (last, first)[way] & (p > 0)

        @pl.when(detour)
        def _():
            rows = (m_rows, h_rows)[phase]
            src = (k_hbm, v_hbm)[tensor].at[1 - way, rows, :, lanes_of(g)]
            remote(
                src, rb.at[g // 3, phase, tensor], zs.at[phase, way, tensor, g], rr.at[g // 3, phase, tensor],
                (base + nz * p + (0, nz - 1)[way], h),
            ).start()

        @pl.when(jnp.logical_not(detour))
        def _():
            z_copy(phase, way, tensor, g).start()

    def relay_copy(phase, tensor, g):
        rows = (m_rows, h_rows)[phase]
        return remote(
            rb.at[g // 3, phase, tensor], kv.at[tensor, 3 * slot_way, rows, :, lanes_of(g)],
            rs.at[g // 3, phase, tensor], zr.at[phase, slot_way, tensor, g], (target, h),
        )

    def relay_incoming(phase, tensor, g):
        slot = rb.at[g // 3, phase, tensor]
        return remote(slot, slot, rs.at[g // 3, phase, tensor], rr.at[g // 3, phase, tensor], (target, h))

    def relay_step(phase, g):
        if relayed:
            @pl.when(relay & (g % 3 == y))
            def _():
                for tensor in range(2):
                    relay_incoming(phase, tensor, g).wait_recv()
                    relay_copy(phase, tensor, g).start()

    def asm_copy(part, g):
        fr_ = part_frames[part]
        return remote(
            kv.at[1 - core, fr_, m_rows, :, lanes_of(g)], asm.at[fr_, :, :, lanes_of(g)],
            asend.at[part, g], arecv.at[part, g], buddy,
        )

    def x_copy(part, g):
        fr_ = part_frames[part]
        return remote(
            mo.at[fr_, :, :, lanes_of(g)], hb.at[core, fr_, 0:8, :, lanes_of(g)],
            ms.at[part, g], mr.at[part, g], across,
        )

    def fwd_copy(part, g):
        fr_ = part_frames[part]
        return remote(
            hb.at[core, fr_, 0:8, :, lanes_of(g)], hb.at[core, fr_, 0:8, :, lanes_of(g)],
            fs.at[part, g], fr.at[part, g], buddy,
        )

    def halo_copy(part, g):
        fr_ = part_frames[part]
        return remote(
            kv.at[:, fr_, h_rows, :, lanes_of(g)], hb.at[:, fr_, 8:16, :, lanes_of(g)],
            hs.at[part, g], hr.at[part, g], buddy,
        )

    def assemble(part, g):
        for frame in ((1, 2), (0,), (3,))[part]:
            for j in range(8):
                ours = (s_row <= j).astype(jnp.int32) == core
                mine = kv[core, frame, 8 * core + j, :, lanes_of(g)]
                mo[frame, j, :, lanes_of(g)] = jnp.where(ours, mine, asm[frame, j, :, lanes_of(g)])

    loads[0].wait()
    loads[1].wait()

    @pl.loop(0, chunks)
    def _(g):
        asm_copy(0, g).start()

    @pl.loop(0, chunks + lag)
    def _(i):
        @pl.when(i < chunks)
        def _():
            for way in range(2):
                for tensor in range(2):
                    z_start(0, way, tensor, i)

        @pl.when(i >= lag)
        def _():
            for way in range(2):
                for tensor in range(2):
                    z_start(1, way, tensor, i - lag)

    @pl.loop(0, chunks)
    def _(g):
        halo_copy(0, g).start()

    qi = lax.broadcasted_iota(jnp.int32, (128, 256), 0)
    ki = lax.broadcasted_iota(jnp.int32, (128, 256), 1)
    q_win = ((qi % 16 - s_col + 16) % 16) // 8
    k_win = ((ki % 16 - s_col + 16) % 16) // 8
    colbias[...] = jnp.where(q_win == k_win, 0.0, NEG)
    q_low = (qi // 16 >= s_row).astype(jnp.int32)
    k_low = (ki % 128 // 16 >= s_row).astype(jnp.int32)
    same[...] = (q_low == k_low).astype(jnp.float32)

    def pack_and_send(part, g):
        asm_copy(part, g).wait_recv()
        assemble(part, g)
        x_copy(part, g).start()

    @pl.loop(0, lead)
    def _(g):
        pack_and_send(0, g)

    loads[2].wait()

    low = [s_row <= j for j in range(8)]

    def slots(ref, lead, picks, lanes):
        return [
            jnp.where(pick, ref[(*lead, j, slice(None), lanes)], ref[(*lead, 8 + j, slice(None), lanes)])
            for j, pick in enumerate(picks)
        ]

    r_one = low
    r_two = [s_row > j for j in range(8)]
    r_halo = [(s_row <= j).astype(jnp.int32) != core for j in range(8)]

    def weights_of(scores):
        z = scores * SCALE + colbias[...]
        e = jnp.exp2(z - jnp.max(z, axis=1, keepdims=True))
        return e, 1.0 / jnp.sum(e, axis=1, keepdims=True)

    def dot_t(a, b):
        return lax.dot_general(a, b, (((1,), (1,)), ((), ())), preferred_element_type=jnp.float32)

    def dot(a, b):
        return jnp.dot(a, b, preferred_element_type=jnp.float32)

    def attend(frame, lanes):
        frames = (0, 1) if frame == 0 else (2, 3)

        def keys(ref, tensor, rows):
            return jnp.concatenate([x for f in frames for x in slots(ref, (tensor, f), rows, lanes)], axis=0)

        q_one = jnp.concatenate(slots(q, (frame,), r_one, lanes), axis=0)
        e, inv = weights_of(dot_t(q_one, keys(kv, 0, r_one)))
        one = (dot(e.astype(jnp.bfloat16), keys(kv, 1, r_one)) * inv).astype(jnp.bfloat16)

        q_two = jnp.concatenate(slots(q, (frame,), r_two, lanes), axis=0)
        pick = same[...] > 0.5
        e, inv = weights_of(
            jnp.where(pick, dot_t(q_two, keys(kv, 0, r_two)), dot_t(q_two, keys(hb, 0, r_halo)))
        )
        near = jnp.where(pick, e, 0.0).astype(jnp.bfloat16)
        far = jnp.where(pick, 0.0, e).astype(jnp.bfloat16)
        two = ((dot(near, keys(kv, 1, r_two)) + dot(far, keys(hb, 1, r_halo))) * inv).astype(jnp.bfloat16)
        for j in range(8):
            a = one[16 * j : 16 * j + 16]
            b = two[16 * j : 16 * j + 16]
            ob[frame, j] = jnp.where(low[j], a, b)
            ob[frame, 8 + j] = jnp.where(low[j], b, a)

    def convolve(lanes, mixed_lanes):
        keep_frame = (t > 0, None, None, t < nt - 1)
        for f in range(4):
            top = hb[1, f, 7 + 8 * core, :, lanes].astype(jnp.float32)
            bottom = hb[1, f, 8 - 8 * core, :, lanes].astype(jnp.float32)
            body = kv[1, f, :, :, lanes].astype(jnp.float32)
            top = jnp.where(h > 0, top, 0.0)
            bottom = jnp.where(h < 3, bottom, 0.0)
            if keep_frame[f] is not None:
                top = jnp.where(keep_frame[f], top, 0.0)
                bottom = jnp.where(keep_frame[f], bottom, 0.0)
                body = jnp.where(keep_frame[f], body, 0.0)
            vext[f, 0] = top
            vext[f, 17] = bottom
            vext[f, 1:17] = body
        col = lax.broadcasted_iota(jnp.int32, (4, 16, 128), 1)
        for f in range(2):
            @pl.loop(0, 4)
            def _(rb):
                sums = [jnp.zeros((4, 16, 128), jnp.float32) for _ in range(3)]
                for dt in range(3):
                    for dr in range(3):
                        slab = vext[f + dt, pl.ds(4 * rb + dr, 4)]
                        for dc in range(3):
                            tap = 9 * dt + 3 * dr + dc
                            sums[dc] = sums[dc] + cw[tap : tap + 1, lanes][None] * slab
                left = jnp.where(col > 0, pltpu.roll(sums[0], 1, 1), 0.0)
                right = jnp.where(col < 15, pltpu.roll(sums[2], 15, 1), 0.0)
                term = sums[1] + left + right
                win = ob[f, pl.ds(4 * rb, 4)].astype(jnp.float32)
                mixed[f, pl.ds(4 * rb, 4), :, mixed_lanes] = (win + term).astype(jnp.bfloat16)

    def out_copy(g):
        return pltpu.make_async_copy(mixed.at[:, :, :, lanes_of(g)], out_hbm.at[:, :, :, lanes_of(g)], osem.at[g])

    for i in range(early):
        relay_step(0, i)
        if i >= lag:
            relay_step(1, i - lag)

    @pl.loop(0, chunks + 3)
    def _(i):
        @pl.when(i + early < chunks)
        def _():
            relay_step(0, i + early)

        @pl.when((i + early >= lag) & (i + early < chunks + lag))
        def _():
            relay_step(1, i + early - lag)

        @pl.when(i < chunks)
        def _():
            for way in range(2):
                for tensor in range(2):
                    z_copy(0, way, tensor, i).wait_recv()
            for part in (1, 2):
                asm_copy(part, i).start()

        @pl.when((i >= 2) & (i < chunks + 2))
        def _():
            g = i - 2
            x_copy(0, g).wait_recv()
            fwd_copy(0, g).start()

        @pl.when((i >= 1) & (i < chunks + 1))
        def _():
            for part in (1, 2):
                pack_and_send(part, i - 1)

        @pl.when(i + lead < chunks)
        def _():
            pack_and_send(0, i + lead)

        @pl.when((i >= 2) & (i < chunks + 2))
        def _():
            g = i - 2
            for way in range(2):
                for tensor in range(2):
                    z_copy(1, way, tensor, g).wait_recv()
            for part in (1, 2):
                halo_copy(part, g).start()

        @pl.when((i >= 2) & (i < chunks + 2))
        def _():
            g = i - 2
            for part in (1, 2):
                x_copy(part, g).wait_recv()
                fwd_copy(part, g).start()

        @pl.when(i >= 3)
        def _():
            g = i - 3
            for part in range(3):
                halo_copy(part, g).wait_recv()
                fwd_copy(part, g).wait_recv()
            for frame in range(2):
                attend(frame, lanes_of(g))
            convolve(lanes_of(g), lanes_of(g))
            out_copy(g).start()

    @pl.loop(0, chunks)
    def _(g):
        for phase in range(2):
            for way in range(2):
                for tensor in range(2):
                    z_copy(phase, way, tensor, g).wait_send()
            if relayed:
                @pl.when(relay & (g % 3 == y))
                def _():
                    for tensor in range(2):
                        relay_copy(phase, tensor, g).wait_send()
        for part in range(3):
            asm_copy(part, g).wait_send()
            x_copy(part, g).wait_send()
            fwd_copy(part, g).wait_send()
            halo_copy(part, g).wait_send()
        out_copy(g).wait()


def body(nt, query_states, key_states, value_states, shifts, conv_kernel, out_weight):
    frames, rows, cols, channels = query_states.shape
    width = out_weight.shape[1]
    heads = channels // HEAD_DIM
    lag = 2
    early = 2
    lead = min(4, heads)
    relayed = nt == 64 and heads % 3 == 0
    any_spec = pl.BlockSpec(memory_space=pl.ANY)
    dma = pltpu.SemaphoreType.DMA
    bf16 = jnp.bfloat16
    mixed = pl.pallas_call(
        functools.partial(kernel, nt, heads, lag, lead, early, relayed),
        out_shape=jax.ShapeDtypeStruct((frames, rows, cols, channels), bf16),
        in_specs=[
            pl.BlockSpec(memory_space=pltpu.SMEM),
            any_spec, any_spec, any_spec,
            pl.BlockSpec(memory_space=pltpu.VMEM),
        ],
        out_specs=any_spec,
        scratch_shapes=[
            pltpu.VMEM((2, 16, 16, channels), bf16),
            pltpu.VMEM((2, 4, 16, 16, channels), bf16),
            pltpu.VMEM((2, 4, 16, 16, channels), bf16),
            pltpu.VMEM((4, 8, 16, channels), bf16),
            pltpu.VMEM((4, 8, 16, channels), bf16),
            pltpu.VMEM((2, 16, 16, channels), bf16),
            pltpu.VMEM((2, 16, 16, HEAD_DIM), bf16),
            pltpu.VMEM((4, 18, 16, HEAD_DIM), jnp.float32),
            pltpu.VMEM((128, 256), jnp.float32),
            pltpu.VMEM((128, 256), jnp.float32),
            pltpu.VMEM((max(1, heads // 3), 2, 2, 8, 16, HEAD_DIM), bf16),
            dma((3,)),
            dma((2, 2, 2, heads)), dma((2, 2, 2, heads)),
            dma((3, heads)), dma((3, heads)),
            dma((3, heads)), dma((3, heads)),
            dma((3, heads)), dma((3, heads)),
            dma((3, heads)), dma((3, heads)),
            dma((max(1, heads // 3), 2, 2)), dma((max(1, heads // 3), 2, 2)),
            dma((heads,)),
        ],
        compiler_params=pltpu.CompilerParams(
            collective_id=0, has_side_effects=True, vmem_limit_bytes=60 * 2**20
        ),
        name="window_block",
    )(shifts, query_states, key_states, value_states, conv_kernel)
    block_out = jnp.dot(
        mixed.reshape(frames * rows * cols, channels), out_weight, preferred_element_type=jnp.float32
    )
    return block_out.astype(bf16).reshape(frames, rows, cols, width)


def solution(mesh):
    in_specs = (
        P("tm", "height", None, None),
        P("tm", "height", None, None),
        P("tm", "height", None, None),
        P(),
        P(),
        P(),
    )
    out_specs = P("tm", "height", None, None)
    return jax.shard_map(
        functools.partial(body, mesh.shape["tm"]), mesh=mesh, in_specs=in_specs, out_specs=out_specs, check_vma=False
    )
```

```python
import functools
import math

import jax
import jax.numpy as jnp
from jax import lax
from jax.experimental import pallas as pl
from jax.experimental.pallas import tpu as pltpu
from jax.sharding import PartitionSpec as P

HEAD_DIM = 128
MESH = pl.DeviceIdType.MESH
NEG = -1e30
GROUP = 4 * HEAD_DIM
TILE = 512
SCALE = math.log2(math.e) / math.sqrt(HEAD_DIM)


def kernel(
    nt, chunks, lag, lead, early, early_heads, relayed,
    shifts, q_hbm, k_hbm, v_hbm, cw_hbm, w_hbm, out_hbm, part_hbm,
    q, kv, hb, asm, mo, mixed, ob, vext, colbias, same, rb, w, acc, cw,
    lsem, zs, zr, asend, arecv, ms, mr, fs, fr, hs, hr, rs, rr, osem, psem,
):
    t = lax.axis_index("tm")
    h = lax.axis_index("height")
    core = lax.rem(h, 2)
    nxt = (lax.rem(t + 1, nt), h)
    prv = (lax.rem(t + nt - 1, nt), h)
    buddy = (t, h + 1 - 2 * core)
    across = (t, lax.rem(h + 2, 4))
    m_rows = pl.ds(8 * core, 8)
    h_rows = pl.ds(8 - 8 * core, 8)
    s_row = shifts[0]
    s_col = shifts[1]

    def lanes_of(g):
        return pl.ds(pl.multiple_of(g * HEAD_DIM, HEAD_DIM), HEAD_DIM)

    def remote(src, dst, ssem, rsem, dev):
        return pltpu.make_async_remote_copy(
            src_ref=src, dst_ref=dst, send_sem=ssem, recv_sem=rsem, device_id=dev, device_id_type=MESH
        )

    loads = [
        pltpu.make_async_copy(k_hbm, kv.at[0, 1:3], lsem.at[0]),
        pltpu.make_async_copy(v_hbm, kv.at[1, 1:3], lsem.at[1]),
        pltpu.make_async_copy(q_hbm, q, lsem.at[2]),
        pltpu.make_async_copy(cw_hbm, cw, lsem.at[3]),
        pltpu.make_async_copy(w_hbm.at[0 : 2 * GROUP], w, lsem.at[4]),
    ]
    for load in loads if early_heads else loads[:4]:
        load.start()

    greet = [(None, dev) for dev in (nxt, prv, buddy, across)]
    if relayed:
        half, nz = nt // 2, nt // 8
        base = t // half * half
        other = half - base
        y = t % half // nz
        first, last = t % half == 0, t % half == half - 1
        middle = (y == 1) | (y == 2)
        relay_up = (t % nz == 0) & middle
        relay_down = (t % nz == nz - 1) & middle
        relay = relay_up | relay_down
        slot_way = jnp.where(relay_up, 0, 1)
        target = jnp.where(relay_up, other, other + half - 1)
        for p in (1, 2):
            greet.append((last, (base + nz * p, h)))
            greet.append((first, (other + nz * p, h)))
            greet.append((first, (base + nz * p + nz - 1, h)))
            greet.append((last, (other + nz * p + nz - 1, h)))
        greet.append((relay_up, (base + half - 1, h)))
        greet.append((relay_up, (other, h)))
        greet.append((relay_down, (base, h)))
        greet.append((relay_down, (other + half - 1, h)))

    bar = pltpu.get_barrier_semaphore()
    met = 0
    for cond, dev in greet:
        if cond is None:
            pl.semaphore_signal(bar, inc=1, device_id=dev, device_id_type=MESH)
            met = met + 1
        else:
            @pl.when(cond)
            def _():
                pl.semaphore_signal(bar, inc=1, device_id=dev, device_id_type=MESH)
            met = met + jnp.where(cond, 1, 0)
    pl.semaphore_wait(bar, met)

    part_frames = (pl.ds(1, 2), pl.ds(0, 1), pl.ds(3, 1))

    def z_copy(phase, way, tensor, g):
        rows = (m_rows, h_rows)[phase]
        src = (k_hbm, v_hbm)[tensor].at[1 - way, rows, :, lanes_of(g)]
        dst = kv.at[tensor, 3 * way, rows, :, lanes_of(g)]
        return remote(src, dst, zs.at[phase, way, tensor, g], zr.at[phase, way, tensor, g], (nxt, prv)[way])

    def z_start(phase, way, tensor, g):
        if not relayed:
            z_copy(phase, way, tensor, g).start()
            return
        p = g % 3
        detour = (last, first)[way] & (p > 0)

        @pl.when(detour)
        def _():
            rows = (m_rows, h_rows)[phase]
            src = (k_hbm, v_hbm)[tensor].at[1 - way, rows, :, lanes_of(g)]
            remote(
                src, rb.at[g // 3, phase, tensor], zs.at[phase, way, tensor, g], rr.at[g // 3, phase, tensor],
                (base + nz * p + (0, nz - 1)[way], h),
            ).start()

        @pl.when(jnp.logical_not(detour))
        def _():
            z_copy(phase, way, tensor, g).start()

    def relay_copy(phase, tensor, g):
        rows = (m_rows, h_rows)[phase]
        return remote(
            rb.at[g // 3, phase, tensor], kv.at[tensor, 3 * slot_way, rows, :, lanes_of(g)],
            rs.at[g // 3, phase, tensor], zr.at[phase, slot_way, tensor, g], (target, h),
        )

    def relay_incoming(phase, tensor, g):
        slot = rb.at[g // 3, phase, tensor]
        return remote(slot, slot, rs.at[g // 3, phase, tensor], rr.at[g // 3, phase, tensor], (target, h))

    def relay_step(phase, g):
        if relayed:
            @pl.when(relay & (g % 3 == y))
            def _():
                for tensor in range(2):
                    relay_incoming(phase, tensor, g).wait_recv()
                    relay_copy(phase, tensor, g).start()

    def asm_copy(part, g):
        fr_ = part_frames[part]
        return remote(
            kv.at[1 - core, fr_, m_rows, :, lanes_of(g)], asm.at[fr_, :, :, lanes_of(g)],
            asend.at[part, g], arecv.at[part, g], buddy,
        )

    def x_copy(part, g):
        fr_ = part_frames[part]
        return remote(
            mo.at[fr_, :, :, lanes_of(g)], hb.at[core, fr_, 0:8, :, lanes_of(g)],
            ms.at[part, g], mr.at[part, g], across,
        )

    def fwd_copy(part, g):
        fr_ = part_frames[part]
        return remote(
            hb.at[core, fr_, 0:8, :, lanes_of(g)], hb.at[core, fr_, 0:8, :, lanes_of(g)],
            fs.at[part, g], fr.at[part, g], buddy,
        )

    def halo_copy(part, g):
        fr_ = part_frames[part]
        return remote(
            kv.at[:, fr_, h_rows, :, lanes_of(g)], hb.at[:, fr_, 8:16, :, lanes_of(g)],
            hs.at[part, g], hr.at[part, g], buddy,
        )

    def assemble(part, g):
        for frame in ((1, 2), (0,), (3,))[part]:
            for j in range(8):
                ours = (s_row <= j).astype(jnp.int32) == core
                mine = kv[core, frame, 8 * core + j, :, lanes_of(g)]
                mo[frame, j, :, lanes_of(g)] = jnp.where(ours, mine, asm[frame, j, :, lanes_of(g)])

    loads[0].wait()
    loads[1].wait()

    @pl.loop(0, chunks)
    def _(g):
        asm_copy(0, g).start()

    def z_issue(i):
        @pl.when(i < chunks)
        def _():
            for way in range(2):
                for tensor in range(2):
                    z_start(0, way, tensor, i)

        @pl.when((i >= lag) & (i < chunks + lag))
        def _():
            for way in range(2):
                for tensor in range(2):
                    z_start(1, way, tensor, i - lag)

    def pack_and_send(part, g):
        asm_copy(part, g).wait_recv()
        assemble(part, g)
        x_copy(part, g).start()

    @pl.loop(0, lead)
    def _(g):
        z_issue(g)
        pack_and_send(0, g)
        halo_copy(0, g).start()

    @pl.loop(lead, chunks + lag)
    def _(i):
        z_issue(i)

    qi = lax.broadcasted_iota(jnp.int32, (128, 256), 0)
    ki = lax.broadcasted_iota(jnp.int32, (128, 256), 1)
    q_win = ((qi % 16 - s_col + 16) % 16) // 8
    k_win = ((ki % 16 - s_col + 16) % 16) // 8
    colbias[...] = jnp.where(q_win == k_win, 0.0, NEG)
    q_low = (qi // 16 >= s_row).astype(jnp.int32)
    k_low = (ki % 128 // 16 >= s_row).astype(jnp.int32)
    same[...] = (q_low == k_low).astype(jnp.float32)

    loads[2].wait()
    loads[3].wait()
    if early_heads:
        loads[4].wait()

    low = [s_row <= j for j in range(8)]

    def slots(ref, lead, picks, lanes):
        return [
            jnp.where(pick, ref[(*lead, j, slice(None), lanes)], ref[(*lead, 8 + j, slice(None), lanes)])
            for j, pick in enumerate(picks)
        ]

    r_one = low
    r_two = [s_row > j for j in range(8)]
    r_halo = [(s_row <= j).astype(jnp.int32) != core for j in range(8)]

    def weights_of(scores):
        z = scores * SCALE + colbias[...]
        e = jnp.exp2(z - jnp.max(z, axis=1, keepdims=True))
        return e, 1.0 / jnp.sum(e, axis=1, keepdims=True)

    def dot_t(a, b):
        return lax.dot_general(a, b, (((1,), (1,)), ((), ())), preferred_element_type=jnp.float32)

    def dot(a, b):
        return jnp.dot(a, b, preferred_element_type=jnp.float32)

    def attend(lanes):
        pick = same[...] > 0.5
        pairs = ((0, 1), (2, 3))

        def keys(ref, tensor, rows, frames):
            return jnp.concatenate([x for f in frames for x in slots(ref, (tensor, f), rows, lanes)], axis=0)

        def queries(frame, rows):
            return jnp.concatenate(slots(q, (frame,), rows, lanes), axis=0)

        scores_one = [dot_t(queries(f, r_one), keys(kv, 0, r_one, pairs[f])) for f in range(2)]
        scores_two = []
        for f in range(2):
            q_two = queries(f, r_two)
            scores_two.append(
                jnp.where(pick, dot_t(q_two, keys(kv, 0, r_two, pairs[f])), dot_t(q_two, keys(hb, 0, r_halo, pairs[f])))
            )
        soft = [weights_of(x) for x in scores_one + scores_two]
        for f in range(2):
            e, inv = soft[f]
            one = (dot(e.astype(jnp.bfloat16), keys(kv, 1, r_one, pairs[f])) * inv).astype(jnp.bfloat16)
            e, inv = soft[2 + f]
            near = jnp.where(pick, e, 0.0).astype(jnp.bfloat16)
            far = jnp.where(pick, 0.0, e).astype(jnp.bfloat16)
            two = (
                (dot(near, keys(kv, 1, r_two, pairs[f])) + dot(far, keys(hb, 1, r_halo, pairs[f]))) * inv
            ).astype(jnp.bfloat16)
            for j in range(8):
                a = one[16 * j : 16 * j + 16]
                b = two[16 * j : 16 * j + 16]
                ob[f, j] = jnp.where(low[j], a, b)
                ob[f, 8 + j] = jnp.where(low[j], b, a)

    def convolve(lanes, mixed_lanes):
        keep_frame = (t > 0, None, None, t < nt - 1)
        for f in range(4):
            top = hb[1, f, 7 + 8 * core, :, lanes].astype(jnp.float32)
            bottom = hb[1, f, 8 - 8 * core, :, lanes].astype(jnp.float32)
            body = kv[1, f, :, :, lanes].astype(jnp.float32)
            top = jnp.where(h > 0, top, 0.0)
            bottom = jnp.where(h < 3, bottom, 0.0)
            if keep_frame[f] is not None:
                top = jnp.where(keep_frame[f], top, 0.0)
                bottom = jnp.where(keep_frame[f], bottom, 0.0)
                body = jnp.where(keep_frame[f], body, 0.0)
            vext[f, 0] = top
            vext[f, 17] = bottom
            vext[f, 1:17] = body
        col = lax.broadcasted_iota(jnp.int32, (4, 16, 128), 1)
        for f in range(2):
            @pl.loop(0, 4)
            def _(rb):
                sums = [jnp.zeros((4, 16, 128), jnp.float32) for _ in range(3)]
                for dt in range(3):
                    for dr in range(3):
                        slab = vext[f + dt, pl.ds(4 * rb + dr, 4)]
                        for dc in range(3):
                            tap = 9 * dt + 3 * dr + dc
                            sums[dc] = sums[dc] + cw[tap : tap + 1, lanes][None] * slab
                left = jnp.where(col > 0, pltpu.roll(sums[0], 1, 1), 0.0)
                right = jnp.where(col < 15, pltpu.roll(sums[2], 15, 1), 0.0)
                term = sums[1] + left + right
                win = ob[f, pl.ds(4 * rb, 4)].astype(jnp.float32)
                mixed[f, pl.ds(4 * rb, 4), :, mixed_lanes] = (win + term).astype(jnp.bfloat16)

    def out_copy(g):
        rest = pl.ds(pl.multiple_of((g - early_heads) * HEAD_DIM, HEAD_DIM), HEAD_DIM)
        return pltpu.make_async_copy(mixed.at[:, :, :, lanes_of(g)], out_hbm.at[:, :, :, rest], osem.at[g])

    third = acc.shape[1] // 3

    def part_copy(k):
        cols = pl.ds(pl.multiple_of(k * third, 128), third)
        return pltpu.make_async_copy(acc.at[:, cols], part_hbm.at[:, cols], psem.at[k])

    def project_early(unit):
        group, k = unit // 3, unit % 3
        lanes = pl.ds(pl.multiple_of(group * GROUP, GROUP), GROUP)
        left = mixed[:, :, :, lanes].reshape(512, GROUP)

        @pl.loop(0, third // TILE)
        def _(i):
            cols = pl.ds(pl.multiple_of(k * third + i * TILE, 128), TILE)
            part = dot(left, w[lanes, cols])

            @pl.when(group == 0)
            def _():
                acc[:, cols] = part

            @pl.when(group == 1)
            def _():
                acc[:, cols] = acc[:, cols] + part

        @pl.when(group == 1)
        def _():
            part_copy(k).start()

    for i in range(early):
        relay_step(0, i)
        if i >= lag:
            relay_step(1, i - lag)

    @pl.loop(0, chunks + 3)
    def _(i):
        @pl.when(i + early < chunks)
        def _():
            relay_step(0, i + early)

        @pl.when((i + early >= lag) & (i + early < chunks + lag))
        def _():
            relay_step(1, i + early - lag)

        @pl.when(i < chunks)
        def _():
            for way in range(2):
                for tensor in range(2):
                    z_copy(0, way, tensor, i).wait_recv()
            for part in (1, 2):
                asm_copy(part, i).start()

        @pl.when((i >= 2) & (i < chunks + 2))
        def _():
            g = i - 2
            x_copy(0, g).wait_recv()
            fwd_copy(0, g).start()

        @pl.when((i >= 1) & (i < chunks + 1))
        def _():
            for part in (1, 2):
                pack_and_send(part, i - 1)

        @pl.when(i + lead < chunks)
        def _():
            pack_and_send(0, i + lead)
            halo_copy(0, i + lead).start()

        @pl.when((i >= 2) & (i < chunks + 2))
        def _():
            g = i - 2
            for way in range(2):
                for tensor in range(2):
                    z_copy(1, way, tensor, g).wait_recv()
            for part in (1, 2):
                halo_copy(part, g).start()

        @pl.when((i >= 2) & (i < chunks + 2))
        def _():
            g = i - 2
            for part in (1, 2):
                x_copy(part, g).wait_recv()
                fwd_copy(part, g).start()

        @pl.when(i >= 3)
        def _():
            g = i - 3
            for part in range(3):
                halo_copy(part, g).wait_recv()
                fwd_copy(part, g).wait_recv()
            attend(lanes_of(g))
            convolve(lanes_of(g), lanes_of(g))

            @pl.when(g >= early_heads)
            def _():
                out_copy(g).start()

        if early_heads:
            @pl.when((i >= 7) & (i < 13))
            def _():
                project_early(i - 7)

    @pl.loop(0, chunks)
    def _(g):
        for phase in range(2):
            for way in range(2):
                for tensor in range(2):
                    z_copy(phase, way, tensor, g).wait_send()
            if relayed:
                @pl.when(relay & (g % 3 == y))
                def _():
                    for tensor in range(2):
                        relay_copy(phase, tensor, g).wait_send()
        for part in range(3):
            asm_copy(part, g).wait_send()
            x_copy(part, g).wait_send()
            fwd_copy(part, g).wait_send()
            halo_copy(part, g).wait_send()

        @pl.when(g >= early_heads)
        def _():
            out_copy(g).wait()

    if early_heads:
        for k in range(3):
            part_copy(k).wait()


def project_late(first_row, late, tiles, x, w, part, out_hbm, out, osem):
    def store(i):
        cols = pl.ds(i * TILE, TILE)
        return pltpu.make_async_copy(out.at[:, cols], out_hbm.at[:, cols], osem.at[i])

    for i in range(tiles):
        cols = pl.ds(i * TILE, TILE)
        late_part = jnp.dot(x[...], w[first_row : first_row + late, cols], preferred_element_type=jnp.float32)
        out[:, cols] = (part[:, cols] + late_part).astype(jnp.bfloat16)
        store(i).start()
    for i in range(tiles):
        store(i).wait()


def body(nt, query_states, key_states, value_states, shifts, conv_kernel, out_weight):
    frames, rows, cols, channels = query_states.shape
    width = out_weight.shape[1]
    heads = channels // HEAD_DIM
    lag = 2
    early = 2
    lead = min(4, heads)
    relayed = nt == 64 and heads % 3 == 0
    any_spec = pl.BlockSpec(memory_space=pl.ANY)
    dma = pltpu.SemaphoreType.DMA
    bf16 = jnp.bfloat16
    early_heads = 8 if heads == 12 else 0
    late = channels - early_heads * HEAD_DIM
    tokens = frames * rows * cols
    operands = [
        pltpu.with_memory_space_constraint(a, pltpu.HBM)
        for a in (shifts, query_states, key_states, value_states, conv_kernel, out_weight)
    ]
    mixed, part = pl.pallas_call(
        functools.partial(kernel, nt, heads, lag, lead, early, early_heads, relayed),
        out_shape=(
            jax.ShapeDtypeStruct((frames, rows, cols, late), bf16),
            jax.ShapeDtypeStruct((tokens, width), jnp.float32),
        ),
        in_specs=[
            pl.BlockSpec(memory_space=pltpu.SMEM),
            any_spec, any_spec, any_spec, any_spec, any_spec,
        ],
        out_specs=(any_spec, any_spec),
        scratch_shapes=[
            pltpu.VMEM((2, 16, 16, channels), bf16),
            pltpu.VMEM((2, 4, 16, 16, channels), bf16),
            pltpu.VMEM((2, 4, 16, 16, channels), bf16),
            pltpu.VMEM((4, 8, 16, channels), bf16),
            pltpu.VMEM((4, 8, 16, channels), bf16),
            pltpu.VMEM((2, 16, 16, channels), bf16),
            pltpu.VMEM((2, 16, 16, HEAD_DIM), bf16),
            pltpu.VMEM((4, 18, 16, HEAD_DIM), jnp.float32),
            pltpu.VMEM((128, 256), jnp.float32),
            pltpu.VMEM((128, 256), jnp.float32),
            pltpu.VMEM((max(1, heads // 3), 2, 2, 8, 16, HEAD_DIM), bf16),
            pltpu.VMEM((early_heads * HEAD_DIM or 16, width), bf16),
            pltpu.VMEM((tokens, width if early_heads else 384), jnp.float32),
            pltpu.VMEM((27, channels), jnp.float32),
            dma((5,)),
            dma((2, 2, 2, heads)), dma((2, 2, 2, heads)),
            dma((3, heads)), dma((3, heads)),
            dma((3, heads)), dma((3, heads)),
            dma((3, heads)), dma((3, heads)),
            dma((3, heads)), dma((3, heads)),
            dma((max(1, heads // 3), 2, 2)), dma((max(1, heads // 3), 2, 2)),
            dma((heads,)),
            dma((3,)),
        ],
        compiler_params=pltpu.CompilerParams(
            collective_id=0, has_side_effects=True, vmem_limit_bytes=40 * 2**20
        ),
        name="window_block",
    )(*operands)
    if not early_heads:
        block_out = jnp.dot(
            mixed.reshape(tokens, channels), out_weight, preferred_element_type=jnp.float32
        )
        return block_out.astype(bf16).reshape(frames, rows, cols, width)
    tiles = width // TILE
    block_out = pl.pallas_call(
        functools.partial(project_late, early_heads * HEAD_DIM, late, tiles),
        out_shape=jax.ShapeDtypeStruct((tokens, width), bf16),
        in_specs=[pl.BlockSpec(memory_space=pltpu.VMEM)] * 3,
        out_specs=any_spec,
        scratch_shapes=[pltpu.VMEM((tokens, width), bf16), dma((tiles,))],
        compiler_params=pltpu.CompilerParams(vmem_limit_bytes=8 * 2**20),
        name="project_late",
    )(mixed.reshape(tokens, late), out_weight, part)
    return block_out.reshape(frames, rows, cols, width)


def solution(mesh):
    in_specs = (
        P("tm", "height", None, None),
        P("tm", "height", None, None),
        P("tm", "height", None, None),
        P(),
        P(),
        P(),
    )
    out_specs = P("tm", "height", None, None)
    return jax.shard_map(
        functools.partial(body, mesh.shape["tm"]), mesh=mesh, in_specs=in_specs, out_specs=out_specs, check_vma=False
    )
```

```python
import functools
import math

import jax
import jax.numpy as jnp
from jax import lax
from jax.experimental import pallas as pl
from jax.experimental.pallas import tpu as pltpu
from jax.sharding import PartitionSpec as P

HEAD_DIM = 128
MESH = pl.DeviceIdType.MESH
NEG = -1e30
GROUP = 4 * HEAD_DIM
TILE = 512
SIDE_FROM = 4
SCALE = math.log2(math.e) / math.sqrt(HEAD_DIM)


def kernel(
    nt, chunks, lag, own_lag, lead, early_heads, relayed,
    shifts, q_hbm, k_hbm, v_hbm, cw_hbm, w_hbm, out_hbm, part_hbm,
    q, kv, hb, asm, mo, mixed, ob, vext, colbias, same, rb, w, acc, cw,
    lsem, zs, zr, asend, arecv, ms, mr, fs, fr, hs, hr, rs, rr, cs, osem, psem,
):
    t = lax.axis_index("tm")
    h = lax.axis_index("height")
    core = lax.rem(h, 2)
    nxt = (lax.rem(t + 1, nt), h)
    prv = (lax.rem(t + nt - 1, nt), h)
    buddy = (t, h + 1 - 2 * core)
    across = (t, lax.rem(h + 2, 4))
    m_rows = pl.ds(8 * core, 8)
    h_rows = pl.ds(8 - 8 * core, 8)
    s_row = shifts[0]
    s_col = shifts[1]

    def lanes_of(g):
        return pl.ds(pl.multiple_of(g * HEAD_DIM, HEAD_DIM), HEAD_DIM)

    def remote(src, dst, ssem, rsem, dev):
        return pltpu.make_async_remote_copy(
            src_ref=src, dst_ref=dst, send_sem=ssem, recv_sem=rsem, device_id=dev, device_id_type=MESH
        )

    loads = [
        pltpu.make_async_copy(k_hbm, kv.at[0, 1:3], lsem.at[0]),
        pltpu.make_async_copy(v_hbm, kv.at[1, 1:3], lsem.at[1]),
        pltpu.make_async_copy(q_hbm, q, lsem.at[2]),
        pltpu.make_async_copy(cw_hbm, cw, lsem.at[3]),
        pltpu.make_async_copy(w_hbm.at[0 : 2 * GROUP], w, lsem.at[4]),
    ]
    for load in loads if early_heads else loads[:4]:
        load.start()

    greet = [(None, dev) for dev in (nxt, prv, buddy, across)]
    if relayed:
        half, nz = nt // 2, nt // 8
        base = t // half * half
        other = half - base
        y = t % half // nz
        first, last = t % half == 0, t % half == half - 1
        middle = (y == 1) | (y == 2)
        relay_up = (t % nz == 0) & middle
        relay_down = (t % nz == nz - 1) & middle
        relay = relay_up | relay_down
        slot_way = jnp.where(relay_up, 0, 1)
        target = jnp.where(relay_up, other, other + half - 1)
        for p in (1, 2):
            greet.append((last, (base + nz * p, h)))
            greet.append((first, (other + nz * p, h)))
            greet.append((first, (base + nz * p + nz - 1, h)))
            greet.append((last, (other + nz * p + nz - 1, h)))
        greet.append((relay_up, (base + half - 1, h)))
        greet.append((relay_up, (other, h)))
        greet.append((relay_down, (base, h)))
        greet.append((relay_down, (other + half - 1, h)))

    def side_in(part, g):
        if not relayed:
            return False
        return (t % nz == (nz - 1 if part == 1 else 0)) & (g >= SIDE_FROM)

    def side_out(way, g):
        return (t % nz == (nz - 2 if way == 0 else 1)) & (g >= SIDE_FROM)

    bar = pltpu.get_barrier_semaphore()
    met = 0
    for cond, dev in greet:
        if cond is None:
            pl.semaphore_signal(bar, inc=1, device_id=dev, device_id_type=MESH)
            met = met + 1
        else:
            @pl.when(cond)
            def _():
                pl.semaphore_signal(bar, inc=1, device_id=dev, device_id_type=MESH)
            met = met + jnp.where(cond, 1, 0)
    pl.semaphore_wait(bar, met)

    part_frames = (pl.ds(1, 2), pl.ds(0, 1), pl.ds(3, 1))

    def z_copy(phase, way, g):
        rows = (m_rows, h_rows)[phase]
        return remote(
            kv.at[:, 2 - way, rows, :, lanes_of(g)], kv.at[:, 3 * way, rows, :, lanes_of(g)],
            zs.at[phase, way, g], zr.at[phase, way, g], (nxt, prv)[way],
        )

    def z_start(phase, way, g):
        if not relayed:
            z_copy(phase, way, g).start()
            return
        p = (g + 0) % 3
        detour = (last, first)[way] & (p > 0)

        @pl.when(detour)
        def _():
            rows = (m_rows, h_rows)[phase]
            remote(
                kv.at[:, 2 - way, rows, :, lanes_of(g)], rb.at[g // 3, phase],
                zs.at[phase, way, g], rr.at[g // 3, phase], (base + nz * p + (0, nz - 1)[way], h),
            ).start()

        @pl.when(jnp.logical_not(detour))
        def _():
            z_copy(phase, way, g).start()

    def relay_copy(phase, g):
        rows = (m_rows, h_rows)[phase]
        return remote(
            rb.at[g // 3, phase], kv.at[:, 3 * slot_way, rows, :, lanes_of(g)],
            rs.at[g // 3, phase], zr.at[phase, slot_way, g], (target, h),
        )

    def relay_incoming(phase, g):
        slot = rb.at[g // 3, phase]
        return remote(slot, slot, rs.at[g // 3, phase], rr.at[g // 3, phase], (target, h))

    def relay_step(phase, g):
        if relayed:
            @pl.when(relay & ((g + 0) % 3 == y))
            def _():
                relay_incoming(phase, g).wait_recv()
                relay_copy(phase, g).start()

    def asm_copy(part, g):
        fr_ = part_frames[part]
        return remote(
            kv.at[1 - core, fr_, m_rows, :, lanes_of(g)], asm.at[fr_, :, :, lanes_of(g)],
            asend.at[part, g], arecv.at[part, g], buddy,
        )

    def x_copy(part, g):
        fr_ = part_frames[part]
        return remote(
            mo.at[fr_, :, :, lanes_of(g)], hb.at[core, fr_, 0:8, :, lanes_of(g)],
            ms.at[part, g], mr.at[part, g], across,
        )

    def side_copy(way, g):
        return remote(
            hb.at[core, pl.ds(2 - way, 1), 0:8, :, lanes_of(g)], hb.at[core, pl.ds(3 * way, 1), 0:8, :, lanes_of(g)],
            cs.at[way, g], mr.at[1 + way, g], (nxt, prv)[way],
        )

    def fwd_copy(part, g):
        fr_ = part_frames[part]
        return remote(
            hb.at[core, fr_, 0:8, :, lanes_of(g)], hb.at[core, fr_, 0:8, :, lanes_of(g)],
            fs.at[part, g], fr.at[part, g], buddy,
        )

    def halo_copy(part, g):
        fr_ = part_frames[part]
        return remote(
            kv.at[:, fr_, h_rows, :, lanes_of(g)], hb.at[:, fr_, 8:16, :, lanes_of(g)],
            hs.at[part, g], hr.at[part, g], buddy,
        )

    def assemble(part, g):
        for frame in ((1, 2), (0,), (3,))[part]:
            for j in range(8):
                ours = (s_row <= j).astype(jnp.int32) == core
                mine = kv[core, frame, 8 * core + j, :, lanes_of(g)]
                mo[frame, j, :, lanes_of(g)] = jnp.where(ours, mine, asm[frame, j, :, lanes_of(g)])

    loads[0].wait()
    loads[1].wait()

    @pl.loop(0, chunks)
    def _(g):
        asm_copy(0, g).start()

    def z_issue(i):
        @pl.when(i < chunks)
        def _():
            for way in range(2):
                z_start(0, way, i)

        @pl.when((i >= lag) & (i < chunks + lag))
        def _():
            for way in range(2):
                z_start(1, way, i - lag)

    def pack_and_send(part, g):
        asm_copy(part, g).wait_recv()
        if part == 0 or not relayed:
            assemble(part, g)
            x_copy(part, g).start()
        else:
            @pl.when(jnp.logical_not(side_in(part, g)))
            def _():
                assemble(part, g)
                x_copy(part, g).start()

    @pl.loop(0, lead)
    def _(g):
        z_issue(g)
        pack_and_send(0, g)
        halo_copy(0, g).start()

    @pl.loop(lead, chunks + lag)
    def _(i):
        z_issue(i)

    qi = lax.broadcasted_iota(jnp.int32, (128, 256), 0)
    ki = lax.broadcasted_iota(jnp.int32, (128, 256), 1)
    q_win = ((qi % 16 - s_col + 16) % 16) // 8
    k_win = ((ki % 16 - s_col + 16) % 16) // 8
    colbias[...] = jnp.where(q_win == k_win, 0.0, NEG)
    q_low = (qi // 16 >= s_row).astype(jnp.int32)
    k_low = (ki % 128 // 16 >= s_row).astype(jnp.int32)
    same[...] = (q_low == k_low).astype(jnp.float32)

    loads[2].wait()
    loads[3].wait()
    if early_heads:
        loads[4].wait()

    low = [s_row <= j for j in range(8)]

    def slots(ref, lead, picks, lanes):
        return [
            jnp.where(pick, ref[(*lead, j, slice(None), lanes)], ref[(*lead, 8 + j, slice(None), lanes)])
            for j, pick in enumerate(picks)
        ]

    r_one = low
    r_two = [s_row > j for j in range(8)]
    r_halo = [(s_row <= j).astype(jnp.int32) != core for j in range(8)]

    def weights_of(scores):
        z = scores * SCALE + colbias[...]
        e = jnp.exp2(z - jnp.max(z, axis=1, keepdims=True))
        return e, 1.0 / jnp.sum(e, axis=1, keepdims=True)

    def dot_t(a, b):
        return lax.dot_general(a, b, (((1,), (1,)), ((), ())), preferred_element_type=jnp.float32)

    def dot(a, b):
        return jnp.dot(a, b, preferred_element_type=jnp.float32)

    def attend(lanes):
        pick = same[...] > 0.5
        pairs = ((0, 1), (2, 3))

        def keys(ref, tensor, rows, frames):
            return jnp.concatenate([x for f in frames for x in slots(ref, (tensor, f), rows, lanes)], axis=0)

        def queries(frame, rows):
            return jnp.concatenate(slots(q, (frame,), rows, lanes), axis=0)

        scores_one = [dot_t(queries(f, r_one), keys(kv, 0, r_one, pairs[f])) for f in range(2)]
        scores_two = []
        for f in range(2):
            q_two = queries(f, r_two)
            scores_two.append(
                jnp.where(pick, dot_t(q_two, keys(kv, 0, r_two, pairs[f])), dot_t(q_two, keys(hb, 0, r_halo, pairs[f])))
            )
        soft = [weights_of(x) for x in scores_one + scores_two]
        for f in range(2):
            e, inv = soft[f]
            one = (dot(e.astype(jnp.bfloat16), keys(kv, 1, r_one, pairs[f])) * inv).astype(jnp.bfloat16)
            e, inv = soft[2 + f]
            near = jnp.where(pick, e, 0.0).astype(jnp.bfloat16)
            far = jnp.where(pick, 0.0, e).astype(jnp.bfloat16)
            two = (
                (dot(near, keys(kv, 1, r_two, pairs[f])) + dot(far, keys(hb, 1, r_halo, pairs[f]))) * inv
            ).astype(jnp.bfloat16)
            for j in range(8):
                a = one[16 * j : 16 * j + 16]
                b = two[16 * j : 16 * j + 16]
                ob[f, j] = jnp.where(low[j], a, b)
                ob[f, 8 + j] = jnp.where(low[j], b, a)

    def convolve(lanes, mixed_lanes):
        keep_frame = (t > 0, None, None, t < nt - 1)
        for f in range(4):
            top = hb[1, f, 7 + 8 * core, :, lanes].astype(jnp.float32)
            bottom = hb[1, f, 8 - 8 * core, :, lanes].astype(jnp.float32)
            body = kv[1, f, :, :, lanes].astype(jnp.float32)
            top = jnp.where(h > 0, top, 0.0)
            bottom = jnp.where(h < 3, bottom, 0.0)
            if keep_frame[f] is not None:
                top = jnp.where(keep_frame[f], top, 0.0)
                bottom = jnp.where(keep_frame[f], bottom, 0.0)
                body = jnp.where(keep_frame[f], body, 0.0)
            vext[f, 0] = top
            vext[f, 17] = bottom
            vext[f, 1:17] = body
        col = lax.broadcasted_iota(jnp.int32, (4, 16, 128), 1)
        for f in range(2):
            @pl.loop(0, 4)
            def _(rb):
                sums = [jnp.zeros((4, 16, 128), jnp.float32) for _ in range(3)]
                for dt in range(3):
                    for dr in range(3):
                        slab = vext[f + dt, pl.ds(4 * rb + dr, 4)]
                        for dc in range(3):
                            tap = 9 * dt + 3 * dr + dc
                            sums[dc] = sums[dc] + cw[tap : tap + 1, lanes][None] * slab
                left = jnp.where(col > 0, pltpu.roll(sums[0], 1, 1), 0.0)
                right = jnp.where(col < 15, pltpu.roll(sums[2], 15, 1), 0.0)
                term = sums[1] + left + right
                win = ob[f, pl.ds(4 * rb, 4)].astype(jnp.float32)
                mixed[f, pl.ds(4 * rb, 4), :, mixed_lanes] = (win + term).astype(jnp.bfloat16)

    def out_copy(g):
        rest = pl.ds(pl.multiple_of((g - early_heads) * HEAD_DIM, HEAD_DIM), HEAD_DIM)
        return pltpu.make_async_copy(mixed.at[:, :, :, lanes_of(g)], out_hbm.at[:, :, :, rest], osem.at[g])

    third = acc.shape[1] // 3

    def part_copy(k):
        cols = pl.ds(pl.multiple_of(k * third, 128), third)
        return pltpu.make_async_copy(acc.at[:, cols], part_hbm.at[:, cols], psem.at[k])

    def project_early(unit):
        group, k = unit // 3, unit % 3
        lanes = pl.ds(pl.multiple_of(group * GROUP, GROUP), GROUP)
        left = mixed[:, :, :, lanes].reshape(512, GROUP)

        @pl.loop(0, third // TILE)
        def _(i):
            cols = pl.ds(pl.multiple_of(k * third + i * TILE, 128), TILE)
            part = dot(left, w[lanes, cols])

            @pl.when(group == 0)
            def _():
                acc[:, cols] = part

            @pl.when(group == 1)
            def _():
                acc[:, cols] = acc[:, cols] + part

        @pl.when(group == 1)
        def _():
            part_copy(k).start()

    def settle(g):
        for phase in range(2):
            for way in range(2):
                z_copy(phase, way, g).wait_send()
            if relayed:
                @pl.when(relay & ((g + 0) % 3 == y))
                def _():
                    relay_copy(phase, g).wait_send()
        for part in range(3):
            asm_copy(part, g).wait_send()
            if part == 0 or not relayed:
                x_copy(part, g).wait_send()
            else:
                @pl.when(jnp.logical_not(side_in(part, g)))
                def _():
                    x_copy(part, g).wait_send()

                @pl.when(side_out(part - 1, g))
                def _():
                    side_copy(part - 1, g).wait_send()
            fwd_copy(part, g).wait_send()
            halo_copy(part, g).wait_send()

        @pl.when(g >= early_heads)
        def _():
            out_copy(g).wait()

    @pl.loop(0, chunks + lag + 1)
    def _(i):
        for more in range(2):
            v = (3 * i + 1) // 2 + more

            @pl.when((2 * v // 3 == i) & (v < chunks))
            def _():
                relay_step(0, v)

            @pl.when((2 * v // 3 == i) & (v >= lag) & (v < chunks + lag))
            def _():
                relay_step(1, v - lag)

        @pl.when(i < chunks)
        def _():
            for way in range(2):
                z_copy(0, way, i).wait_recv()
            for part in (1, 2):
                asm_copy(part, i).start()

        @pl.when((i >= own_lag) & (i < chunks + own_lag))
        def _():
            g = i - own_lag
            x_copy(0, g).wait_recv()
            fwd_copy(0, g).start()
            if relayed:
                for way in range(2):
                    @pl.when(side_out(way, g))
                    def _():
                        side_copy(way, g).start()

        @pl.when((i >= 1) & (i < chunks + 1))
        def _():
            for part in (1, 2):
                pack_and_send(part, i - 1)

        @pl.when(i + lead < chunks)
        def _():
            pack_and_send(0, i + lead)
            halo_copy(0, i + lead).start()

        @pl.when((i >= lag) & (i < chunks + lag))
        def _():
            g = i - lag
            for way in range(2):
                z_copy(1, way, g).wait_recv()
            for part in (1, 2):
                halo_copy(part, g).start()

        @pl.when((i >= lag) & (i < chunks + lag))
        def _():
            g = i - lag
            for part in (1, 2):
                x_copy(part, g).wait_recv()
                fwd_copy(part, g).start()

        @pl.when(i > lag)
        def _():
            g = i - lag - 1
            for part in range(3):
                halo_copy(part, g).wait_recv()
                fwd_copy(part, g).wait_recv()
            attend(lanes_of(g))
            convolve(lanes_of(g), lanes_of(g))

            @pl.when(g >= early_heads)
            def _():
                out_copy(g).start()

        if early_heads:
            for group in range(2):
                first_step = lag + 4 + 4 * group

                @pl.when((i >= first_step) & (i < first_step + 3))
                def _():
                    project_early(3 * group + i - first_step)

        @pl.when(i > lag + 3)
        def _():
            settle(i - lag - 4)

    @pl.loop(max(0, chunks - 3), chunks)
    def _(g):
        settle(g)

    if early_heads:
        for k in range(3):
            part_copy(k).wait()


def project_late(first_row, late, tiles, x, w, part, out_hbm, out, osem):
    def store(i):
        cols = pl.ds(i * TILE, TILE)
        return pltpu.make_async_copy(out.at[:, cols], out_hbm.at[:, cols], osem.at[i])

    for i in range(tiles):
        cols = pl.ds(i * TILE, TILE)
        late_part = jnp.dot(x[...], w[first_row : first_row + late, cols], preferred_element_type=jnp.float32)
        out[:, cols] = (part[:, cols] + late_part).astype(jnp.bfloat16)
        store(i).start()
    for i in range(tiles):
        store(i).wait()


def body(nt, query_states, key_states, value_states, shifts, conv_kernel, out_weight):
    frames, rows, cols, channels = query_states.shape
    width = out_weight.shape[1]
    heads = channels // HEAD_DIM
    lag = min(4, heads)
    own_lag = min(2, heads)
    lead = min(4, heads)
    relayed = nt == 64 and heads % 3 == 0
    any_spec = pl.BlockSpec(memory_space=pl.ANY)
    dma = pltpu.SemaphoreType.DMA
    bf16 = jnp.bfloat16
    early_heads = 8 if heads == 12 else 0
    late = channels - early_heads * HEAD_DIM
    tokens = frames * rows * cols
    operands = [
        pltpu.with_memory_space_constraint(a, pltpu.HBM)
        for a in (shifts, query_states, key_states, value_states, conv_kernel, out_weight)
    ]
    mixed, part = pl.pallas_call(
        functools.partial(kernel, nt, heads, lag, own_lag, lead, early_heads, relayed),
        out_shape=(
            jax.ShapeDtypeStruct((frames, rows, cols, late), bf16),
            jax.ShapeDtypeStruct((tokens, width), jnp.float32),
        ),
        in_specs=[
            pl.BlockSpec(memory_space=pltpu.SMEM),
            any_spec, any_spec, any_spec, any_spec, any_spec,
        ],
        out_specs=(any_spec, any_spec),
        scratch_shapes=[
            pltpu.VMEM((2, 16, 16, channels), bf16),
            pltpu.VMEM((2, 4, 16, 16, channels), bf16),
            pltpu.VMEM((2, 4, 16, 16, channels), bf16),
            pltpu.VMEM((4, 8, 16, channels), bf16),
            pltpu.VMEM((4, 8, 16, channels), bf16),
            pltpu.VMEM((2, 16, 16, channels), bf16),
            pltpu.VMEM((2, 16, 16, HEAD_DIM), bf16),
            pltpu.VMEM((4, 18, 16, HEAD_DIM), jnp.float32),
            pltpu.VMEM((128, 256), jnp.float32),
            pltpu.VMEM((128, 256), jnp.float32),
            pltpu.VMEM((max(1, heads // 3), 2, 2, 8, 16, HEAD_DIM), bf16),
            pltpu.VMEM((early_heads * HEAD_DIM or 16, width), bf16),
            pltpu.VMEM((tokens, width if early_heads else 384), jnp.float32),
            pltpu.VMEM((27, channels), jnp.float32),
            dma((5,)),
            dma((2, 2, heads)), dma((2, 2, heads)),
            dma((3, heads)), dma((3, heads)),
            dma((3, heads)), dma((3, heads)),
            dma((3, heads)), dma((3, heads)),
            dma((3, heads)), dma((3, heads)),
            dma((max(1, heads // 3), 2)), dma((max(1, heads // 3), 2)),
            dma((2, heads)),
            dma((heads,)),
            dma((3,)),
        ],
        compiler_params=pltpu.CompilerParams(
            collective_id=0, has_side_effects=True, vmem_limit_bytes=40 * 2**20
        ),
        name="window_block",
    )(*operands)
    if not early_heads:
        block_out = jnp.dot(
            mixed.reshape(tokens, channels), out_weight, preferred_element_type=jnp.float32
        )
        return block_out.astype(bf16).reshape(frames, rows, cols, width)
    tiles = width // TILE
    block_out = pl.pallas_call(
        functools.partial(project_late, early_heads * HEAD_DIM, late, tiles),
        out_shape=jax.ShapeDtypeStruct((tokens, width), bf16),
        in_specs=[pl.BlockSpec(memory_space=pltpu.VMEM)] * 3,
        out_specs=any_spec,
        scratch_shapes=[pltpu.VMEM((tokens, width), bf16), dma((tiles,))],
        compiler_params=pltpu.CompilerParams(vmem_limit_bytes=8 * 2**20),
        name="project_late",
    )(mixed.reshape(tokens, late), out_weight, part)
    return block_out.reshape(frames, rows, cols, width)


def solution(mesh):
    in_specs = (
        P("tm", "height", None, None),
        P("tm", "height", None, None),
        P("tm", "height", None, None),
        P(),
        P(),
        P(),
    )
    out_specs = P("tm", "height", None, None)
    return jax.shard_map(
        functools.partial(body, mesh.shape["tm"]), mesh=mesh, in_specs=in_specs, out_specs=out_specs, check_vma=False
    )
```

```python
import functools
import math

import jax
import jax.numpy as jnp
from jax import lax
from jax.experimental import pallas as pl
from jax.experimental.pallas import tpu as pltpu
from jax.sharding import PartitionSpec as P

HEAD_DIM = 128
MESH = pl.DeviceIdType.MESH
NEG = -1e30
GROUP = 4 * HEAD_DIM
TILE = 512
SIDE_FROM = 4
SCALE = math.log2(math.e) / math.sqrt(HEAD_DIM)


def kernel(
    nt, chunks, lag, own_lag, lead, early_heads, relayed,
    shifts, q_hbm, k_hbm, v_hbm, cw_hbm, w_hbm, out_hbm, part_hbm,
    q, kv, hb, asm, mo, mixed, ob, vext, colbias, same, rb, w, acc, cw,
    lsem, zs, zr, asend, arecv, ms, mr, fs, fr, hs, hr, rs, rr, cs, osem, psem,
):
    t = lax.axis_index("tm")
    h = lax.axis_index("height")
    core = lax.rem(h, 2)
    nxt = (lax.rem(t + 1, nt), h)
    prv = (lax.rem(t + nt - 1, nt), h)
    buddy = (t, h + 1 - 2 * core)
    across = (t, lax.rem(h + 2, 4))
    m_rows = pl.ds(8 * core, 8)
    h_rows = pl.ds(8 - 8 * core, 8)
    s_row = shifts[0]
    s_col = shifts[1]

    def lanes_of(g):
        return pl.ds(pl.multiple_of(g * HEAD_DIM, HEAD_DIM), HEAD_DIM)

    def remote(src, dst, ssem, rsem, dev):
        return pltpu.make_async_remote_copy(
            src_ref=src, dst_ref=dst, send_sem=ssem, recv_sem=rsem, device_id=dev, device_id_type=MESH
        )

    loads = [
        pltpu.make_async_copy(k_hbm, kv.at[0, 1:3], lsem.at[0]),
        pltpu.make_async_copy(v_hbm, kv.at[1, 1:3], lsem.at[1]),
        pltpu.make_async_copy(q_hbm, q, lsem.at[2]),
        pltpu.make_async_copy(cw_hbm, cw, lsem.at[3]),
        pltpu.make_async_copy(w_hbm.at[0 : 2 * GROUP], w, lsem.at[4]),
    ]
    for load in loads if early_heads else loads[:4]:
        load.start()

    greet = [(None, dev) for dev in (nxt, prv, buddy, across)]
    if relayed:
        half, nz = nt // 2, nt // 8
        base = t // half * half
        other = half - base
        y = t % half // nz
        first, last = t % half == 0, t % half == half - 1
        middle = (y == 1) | (y == 2)
        relay_up = (t % nz == 0) & middle
        relay_down = (t % nz == nz - 1) & middle
        relay = relay_up | relay_down
        slot_way = jnp.where(relay_up, 0, 1)
        target = jnp.where(relay_up, other, other + half - 1)
        for p in (1, 2):
            greet.append((last, (base + nz * p, h)))
            greet.append((first, (other + nz * p, h)))
            greet.append((first, (base + nz * p + nz - 1, h)))
            greet.append((last, (other + nz * p + nz - 1, h)))
        greet.append((relay_up, (base + half - 1, h)))
        greet.append((relay_up, (other, h)))
        greet.append((relay_down, (base, h)))
        greet.append((relay_down, (other + half - 1, h)))

    def side_in(part, g):
        if not relayed:
            return False
        return (t % nz == (nz - 1 if part == 1 else 0)) & (g >= SIDE_FROM)

    def side_out(way, g):
        return (t % nz == (nz - 2 if way == 0 else 1)) & (g >= SIDE_FROM)

    bar = pltpu.get_barrier_semaphore()
    met = 0
    for cond, dev in greet:
        if cond is None:
            pl.semaphore_signal(bar, inc=1, device_id=dev, device_id_type=MESH)
            met = met + 1
        else:
            @pl.when(cond)
            def _():
                pl.semaphore_signal(bar, inc=1, device_id=dev, device_id_type=MESH)
            met = met + jnp.where(cond, 1, 0)
    pl.semaphore_wait(bar, met)

    part_frames = (pl.ds(1, 2), pl.ds(0, 1), pl.ds(3, 1))

    def z_copy(phase, way, g):
        rows = (m_rows, h_rows)[phase]
        return remote(
            kv.at[:, 2 - way, rows, :, lanes_of(g)], kv.at[:, 3 * way, rows, :, lanes_of(g)],
            zs.at[phase, way, g], zr.at[phase, way, g], (nxt, prv)[way],
        )

    def z_start(phase, way, g):
        if not relayed:
            z_copy(phase, way, g).start()
            return
        p = (g + 0) % 3
        detour = (last, first)[way] & (p > 0)

        @pl.when(detour)
        def _():
            rows = (m_rows, h_rows)[phase]
            remote(
                kv.at[:, 2 - way, rows, :, lanes_of(g)], rb.at[g // 3, phase],
                zs.at[phase, way, g], rr.at[g // 3, phase], (base + nz * p + (0, nz - 1)[way], h),
            ).start()

        @pl.when(jnp.logical_not(detour))
        def _():
            z_copy(phase, way, g).start()

    def relay_copy(phase, g):
        rows = (m_rows, h_rows)[phase]
        return remote(
            rb.at[g // 3, phase], kv.at[:, 3 * slot_way, rows, :, lanes_of(g)],
            rs.at[g // 3, phase], zr.at[phase, slot_way, g], (target, h),
        )

    def relay_incoming(phase, g):
        slot = rb.at[g // 3, phase]
        return remote(slot, slot, rs.at[g // 3, phase], rr.at[g // 3, phase], (target, h))

    def relay_step(phase, g):
        if relayed:
            @pl.when(relay & ((g + 0) % 3 == y))
            def _():
                relay_incoming(phase, g).wait_recv()
                relay_copy(phase, g).start()

    def asm_copy(part, g):
        fr_ = part_frames[part]
        return remote(
            kv.at[1 - core, fr_, m_rows, :, lanes_of(g)], asm.at[fr_, :, :, lanes_of(g)],
            asend.at[part, g], arecv.at[part, g], buddy,
        )

    def x_copy(part, g):
        fr_ = part_frames[part]
        return remote(
            mo.at[fr_, :, :, lanes_of(g)], hb.at[core, fr_, 0:8, :, lanes_of(g)],
            ms.at[part, g], mr.at[part, g], across,
        )

    def side_copy(way, g):
        return remote(
            hb.at[core, pl.ds(2 - way, 1), 0:8, :, lanes_of(g)], hb.at[core, pl.ds(3 * way, 1), 0:8, :, lanes_of(g)],
            cs.at[way, g], mr.at[1 + way, g], (nxt, prv)[way],
        )

    def fwd_copy(part, g):
        fr_ = part_frames[part]
        return remote(
            hb.at[core, fr_, 0:8, :, lanes_of(g)], hb.at[core, fr_, 0:8, :, lanes_of(g)],
            fs.at[part, g], fr.at[part, g], buddy,
        )

    def halo_copy(part, g):
        fr_ = part_frames[part]
        return remote(
            kv.at[:, fr_, h_rows, :, lanes_of(g)], hb.at[:, fr_, 8:16, :, lanes_of(g)],
            hs.at[part, g], hr.at[part, g], buddy,
        )

    def assemble(part, g):
        for frame in ((1, 2), (0,), (3,))[part]:
            for j in range(8):
                ours = (s_row <= j).astype(jnp.int32) == core
                mine = kv[core, frame, 8 * core + j, :, lanes_of(g)]
                mo[frame, j, :, lanes_of(g)] = jnp.where(ours, mine, asm[frame, j, :, lanes_of(g)])

    loads[0].wait()
    loads[1].wait()

    @pl.loop(0, chunks)
    def _(g):
        asm_copy(0, g).start()

    def z_issue(i):
        @pl.when(i < chunks)
        def _():
            for way in range(2):
                z_start(0, way, i)

        @pl.when((i >= lag) & (i < chunks + lag))
        def _():
            for way in range(2):
                z_start(1, way, i - lag)

    def pack_and_send(part, g):
        asm_copy(part, g).wait_recv()
        if part == 0 or not relayed:
            assemble(part, g)
            x_copy(part, g).start()
        else:
            @pl.when(jnp.logical_not(side_in(part, g)))
            def _():
                assemble(part, g)
                x_copy(part, g).start()

    @pl.loop(0, lead)
    def _(g):
        z_issue(g)
        pack_and_send(0, g)
        halo_copy(0, g).start()

    paced = False
    if relayed:
        paced = (t % nz == 1) | (t % nz == nz - 2)

    @pl.when(jnp.logical_not(paced))
    def _():
        @pl.loop(lead, chunks + lag)
        def _(i):
            z_issue(i)


    qi = lax.broadcasted_iota(jnp.int32, (128, 256), 0)
    ki = lax.broadcasted_iota(jnp.int32, (128, 256), 1)
    q_win = ((qi % 16 - s_col + 16) % 16) // 8
    k_win = ((ki % 16 - s_col + 16) % 16) // 8
    colbias[...] = jnp.where(q_win == k_win, 0.0, NEG)
    q_low = (qi // 16 >= s_row).astype(jnp.int32)
    k_low = (ki % 128 // 16 >= s_row).astype(jnp.int32)
    same[...] = (q_low == k_low).astype(jnp.float32)

    loads[2].wait()
    loads[3].wait()
    if early_heads:
        loads[4].wait()

    low = [s_row <= j for j in range(8)]

    def slots(ref, lead, picks, lanes):
        return [
            jnp.where(pick, ref[(*lead, j, slice(None), lanes)], ref[(*lead, 8 + j, slice(None), lanes)])
            for j, pick in enumerate(picks)
        ]

    r_one = low
    r_two = [s_row > j for j in range(8)]
    r_halo = [(s_row <= j).astype(jnp.int32) != core for j in range(8)]

    def weights_of(scores):
        z = scores * SCALE + colbias[...]
        e = jnp.exp2(z - jnp.max(z, axis=1, keepdims=True))
        return e, 1.0 / jnp.sum(e, axis=1, keepdims=True)

    def dot_t(a, b):
        return lax.dot_general(a, b, (((1,), (1,)), ((), ())), preferred_element_type=jnp.float32)

    def dot(a, b):
        return jnp.dot(a, b, preferred_element_type=jnp.float32)

    def attend(lanes):
        pick = same[...] > 0.5
        pairs = ((0, 1), (2, 3))

        def keys(ref, tensor, rows, frames):
            return jnp.concatenate([x for f in frames for x in slots(ref, (tensor, f), rows, lanes)], axis=0)

        def queries(frame, rows):
            return jnp.concatenate(slots(q, (frame,), rows, lanes), axis=0)

        scores_one = [dot_t(queries(f, r_one), keys(kv, 0, r_one, pairs[f])) for f in range(2)]
        scores_two = []
        for f in range(2):
            q_two = queries(f, r_two)
            scores_two.append(
                jnp.where(pick, dot_t(q_two, keys(kv, 0, r_two, pairs[f])), dot_t(q_two, keys(hb, 0, r_halo, pairs[f])))
            )
        soft = [weights_of(x) for x in scores_one + scores_two]
        for f in range(2):
            e, inv = soft[f]
            one = (dot(e.astype(jnp.bfloat16), keys(kv, 1, r_one, pairs[f])) * inv).astype(jnp.bfloat16)
            e, inv = soft[2 + f]
            near = jnp.where(pick, e, 0.0).astype(jnp.bfloat16)
            far = jnp.where(pick, 0.0, e).astype(jnp.bfloat16)
            two = (
                (dot(near, keys(kv, 1, r_two, pairs[f])) + dot(far, keys(hb, 1, r_halo, pairs[f]))) * inv
            ).astype(jnp.bfloat16)
            for j in range(8):
                a = one[16 * j : 16 * j + 16]
                b = two[16 * j : 16 * j + 16]
                ob[f, j] = jnp.where(low[j], a, b)
                ob[f, 8 + j] = jnp.where(low[j], b, a)

    def convolve(lanes, mixed_lanes):
        keep_frame = (t > 0, None, None, t < nt - 1)
        for f in range(4):
            top = hb[1, f, 7 + 8 * core, :, lanes].astype(jnp.float32)
            bottom = hb[1, f, 8 - 8 * core, :, lanes].astype(jnp.float32)
            body = kv[1, f, :, :, lanes].astype(jnp.float32)
            top = jnp.where(h > 0, top, 0.0)
            bottom = jnp.where(h < 3, bottom, 0.0)
            if keep_frame[f] is not None:
                top = jnp.where(keep_frame[f], top, 0.0)
                bottom = jnp.where(keep_frame[f], bottom, 0.0)
                body = jnp.where(keep_frame[f], body, 0.0)
            vext[f, 0] = top
            vext[f, 17] = bottom
            vext[f, 1:17] = body
        col = lax.broadcasted_iota(jnp.int32, (4, 16, 128), 1)
        for f in range(2):
            @pl.loop(0, 4)
            def _(rb):
                sums = [jnp.zeros((4, 16, 128), jnp.float32) for _ in range(3)]
                for dt in range(3):
                    for dr in range(3):
                        slab = vext[f + dt, pl.ds(4 * rb + dr, 4)]
                        for dc in range(3):
                            tap = 9 * dt + 3 * dr + dc
                            sums[dc] = sums[dc] + cw[tap : tap + 1, lanes][None] * slab
                left = jnp.where(col > 0, pltpu.roll(sums[0], 1, 1), 0.0)
                right = jnp.where(col < 15, pltpu.roll(sums[2], 15, 1), 0.0)
                term = sums[1] + left + right
                win = ob[f, pl.ds(4 * rb, 4)].astype(jnp.float32)
                mixed[f, pl.ds(4 * rb, 4), :, mixed_lanes] = (win + term).astype(jnp.bfloat16)

    def out_copy(g):
        rest = pl.ds(pl.multiple_of((g - early_heads) * HEAD_DIM, HEAD_DIM), HEAD_DIM)
        return pltpu.make_async_copy(mixed.at[:, :, :, lanes_of(g)], out_hbm.at[:, :, :, rest], osem.at[g])

    third = acc.shape[1] // 3

    def part_copy(k):
        cols = pl.ds(pl.multiple_of(k * third, 128), third)
        return pltpu.make_async_copy(acc.at[:, cols], part_hbm.at[:, cols], psem.at[k])

    def project_early(unit):
        group, k = unit // 3, unit % 3
        lanes = pl.ds(pl.multiple_of(group * GROUP, GROUP), GROUP)
        left = mixed[:, :, :, lanes].reshape(512, GROUP)

        @pl.loop(0, third // TILE)
        def _(i):
            cols = pl.ds(pl.multiple_of(k * third + i * TILE, 128), TILE)
            part = dot(left, w[lanes, cols])

            @pl.when(group == 0)
            def _():
                acc[:, cols] = part

            @pl.when(group == 1)
            def _():
                acc[:, cols] = acc[:, cols] + part

        @pl.when(group == 1)
        def _():
            part_copy(k).start()

    def settle(g):
        for phase in range(2):
            for way in range(2):
                z_copy(phase, way, g).wait_send()
            if relayed:
                @pl.when(relay & ((g + 0) % 3 == y))
                def _():
                    relay_copy(phase, g).wait_send()
        for part in range(3):
            asm_copy(part, g).wait_send()
            if part == 0 or not relayed:
                x_copy(part, g).wait_send()
            else:
                @pl.when(jnp.logical_not(side_in(part, g)))
                def _():
                    x_copy(part, g).wait_send()

                @pl.when(side_out(part - 1, g))
                def _():
                    side_copy(part - 1, g).wait_send()
            fwd_copy(part, g).wait_send()
            halo_copy(part, g).wait_send()

        @pl.when(g >= early_heads)
        def _():
            out_copy(g).wait()

    @pl.loop(0, chunks + lag + 1)
    def _(i):
        for more in range(2):
            v = (3 * i + 1) // 2 + more

            @pl.when((2 * v // 3 == i) & (v < chunks))
            def _():
                relay_step(0, v)

            @pl.when((2 * v // 3 == i) & (v >= lag) & (v < chunks + lag))
            def _():
                relay_step(1, v - lag)

        @pl.when(i < chunks)
        def _():
            for way in range(2):
                z_copy(0, way, i).wait_recv()
            for part in (1, 2):
                asm_copy(part, i).start()

        @pl.when((i >= own_lag) & (i < chunks + own_lag))
        def _():
            g = i - own_lag
            x_copy(0, g).wait_recv()
            fwd_copy(0, g).start()
            if relayed:
                for way in range(2):
                    @pl.when(side_out(way, g))
                    def _():
                        side_copy(way, g).start()

        @pl.when((i >= 1) & (i < chunks + 1))
        def _():
            for part in (1, 2):
                pack_and_send(part, i - 1)

        @pl.when(paced & (i + lead < chunks + lag))
        def _():
            z_issue(i + lead)

        @pl.when(i + lead < chunks)
        def _():
            pack_and_send(0, i + lead)
            halo_copy(0, i + lead).start()

        @pl.when((i >= lag) & (i < chunks + lag))
        def _():
            g = i - lag
            for way in range(2):
                z_copy(1, way, g).wait_recv()
            for part in (1, 2):
                halo_copy(part, g).start()

        @pl.when((i >= lag) & (i < chunks + lag))
        def _():
            g = i - lag
            for part in (1, 2):
                x_copy(part, g).wait_recv()
                fwd_copy(part, g).start()

        @pl.when(i > lag)
        def _():
            g = i - lag - 1
            for part in range(3):
                halo_copy(part, g).wait_recv()
                fwd_copy(part, g).wait_recv()
            attend(lanes_of(g))
            convolve(lanes_of(g), lanes_of(g))

            @pl.when(g >= early_heads)
            def _():
                out_copy(g).start()

        if early_heads:
            for group in range(2):
                first_step = lag + 4 + 4 * group

                @pl.when((i >= first_step) & (i < first_step + 3))
                def _():
                    project_early(3 * group + i - first_step)

        @pl.when(i > lag + 3)
        def _():
            settle(i - lag - 4)

    @pl.loop(max(0, chunks - 3), chunks)
    def _(g):
        settle(g)

    if early_heads:
        for k in range(3):
            part_copy(k).wait()


def project_late(first_row, late, tiles, x, w, part, out_hbm, out, osem):
    def store(i):
        cols = pl.ds(i * TILE, TILE)
        return pltpu.make_async_copy(out.at[:, cols], out_hbm.at[:, cols], osem.at[i])

    for i in range(tiles):
        cols = pl.ds(i * TILE, TILE)
        late_part = jnp.dot(x[...], w[first_row : first_row + late, cols], preferred_element_type=jnp.float32)
        out[:, cols] = (part[:, cols] + late_part).astype(jnp.bfloat16)
        store(i).start()
    for i in range(tiles):
        store(i).wait()


def body(nt, query_states, key_states, value_states, shifts, conv_kernel, out_weight):
    frames, rows, cols, channels = query_states.shape
    width = out_weight.shape[1]
    heads = channels // HEAD_DIM
    lag = min(4, heads)
    own_lag = min(2, heads)
    lead = min(4, heads)
    relayed = nt == 64 and heads % 3 == 0
    any_spec = pl.BlockSpec(memory_space=pl.ANY)
    dma = pltpu.SemaphoreType.DMA
    bf16 = jnp.bfloat16
    early_heads = 8 if heads == 12 else 0
    late = channels - early_heads * HEAD_DIM
    tokens = frames * rows * cols
    operands = [
        pltpu.with_memory_space_constraint(a, pltpu.HBM)
        for a in (shifts, query_states, key_states, value_states, conv_kernel, out_weight)
    ]
    mixed, part = pl.pallas_call(
        functools.partial(kernel, nt, heads, lag, own_lag, lead, early_heads, relayed),
        out_shape=(
            jax.ShapeDtypeStruct((frames, rows, cols, late), bf16),
            jax.ShapeDtypeStruct((tokens, width), jnp.float32),
        ),
        in_specs=[
            pl.BlockSpec(memory_space=pltpu.SMEM),
            any_spec, any_spec, any_spec, any_spec, any_spec,
        ],
        out_specs=(any_spec, any_spec),
        scratch_shapes=[
            pltpu.VMEM((2, 16, 16, channels), bf16),
            pltpu.VMEM((2, 4, 16, 16, channels), bf16),
            pltpu.VMEM((2, 4, 16, 16, channels), bf16),
            pltpu.VMEM((4, 8, 16, channels), bf16),
            pltpu.VMEM((4, 8, 16, channels), bf16),
            pltpu.VMEM((2, 16, 16, channels), bf16),
            pltpu.VMEM((2, 16, 16, HEAD_DIM), bf16),
            pltpu.VMEM((4, 18, 16, HEAD_DIM), jnp.float32),
            pltpu.VMEM((128, 256), jnp.float32),
            pltpu.VMEM((128, 256), jnp.float32),
            pltpu.VMEM((max(1, heads // 3), 2, 2, 8, 16, HEAD_DIM), bf16),
            pltpu.VMEM((early_heads * HEAD_DIM or 16, width), bf16),
            pltpu.VMEM((tokens, width if early_heads else 384), jnp.float32),
            pltpu.VMEM((27, channels), jnp.float32),
            dma((5,)),
            dma((2, 2, heads)), dma((2, 2, heads)),
            dma((3, heads)), dma((3, heads)),
            dma((3, heads)), dma((3, heads)),
            dma((3, heads)), dma((3, heads)),
            dma((3, heads)), dma((3, heads)),
            dma((max(1, heads // 3), 2)), dma((max(1, heads // 3), 2)),
            dma((2, heads)),
            dma((heads,)),
            dma((3,)),
        ],
        compiler_params=pltpu.CompilerParams(
            collective_id=0, has_side_effects=True, vmem_limit_bytes=40 * 2**20
        ),
        name="window_block",
    )(*operands)
    if not early_heads:
        block_out = jnp.dot(
            mixed.reshape(tokens, channels), out_weight, preferred_element_type=jnp.float32
        )
        return block_out.astype(bf16).reshape(frames, rows, cols, width)
    tiles = width // TILE
    block_out = pl.pallas_call(
        functools.partial(project_late, early_heads * HEAD_DIM, late, tiles),
        out_shape=jax.ShapeDtypeStruct((tokens, width), bf16),
        in_specs=[pl.BlockSpec(memory_space=pltpu.VMEM)] * 3,
        out_specs=any_spec,
        scratch_shapes=[pltpu.VMEM((tokens, width), bf16), dma((tiles,))],
        compiler_params=pltpu.CompilerParams(vmem_limit_bytes=8 * 2**20),
        name="project_late",
    )(mixed.reshape(tokens, late), out_weight, part)
    return block_out.reshape(frames, rows, cols, width)


def solution(mesh):
    in_specs = (
        P("tm", "height", None, None),
        P("tm", "height", None, None),
        P("tm", "height", None, None),
        P(),
        P(),
        P(),
    )
    out_specs = P("tm", "height", None, None)
    return jax.shard_map(
        functools.partial(body, mesh.shape["tm"]), mesh=mesh, in_specs=in_specs, out_specs=out_specs, check_vma=False
    )
```
